32 devices in a mesh: trip: 8 (over z, y), row: 4 (over x, core).
Axes of the slice: x: 2, y: 2, z: 4, core: 2. Of those that a mesh axis runs over, the one named last changes fastest.
Arguments:
- eigvecs: bfloat16 [2048, 64, 128], P(('trip', 'row')), may hold values from -0.5 to 0.5
- cubic: bfloat16 [768, 64, 4096], P(('trip', 'row')), may hold values from -0.09375 to 0.09375
- triplets: int32 [768, 3], P(('trip', 'row')), may hold values from 0 to 2047, as said below
- weights: int32 [768], P(('trip', 'row')), may hold values from 1 to 6
- deviation: float32 [2048, 768], P(('trip', 'row')), may hold values from -6 to 6
- source: float32 [2048, 768], P(('trip', 'row')), may hold values from -6 to 6
- base_rate: float32 [2048, 64], P(('trip', 'row')), may hold values from 0.5 to 2
Outputs:
- relaxed: float32 [2048, 768], P(('trip', 'row'))
The draws below stay inside these ranges and needn't reach their ends.
Inputs may be any that keep to these rules, and one draw needn't show every extreme that they name: Column 0 of a device's triplets names wavevectors homed on devices of its own trip group; at most 12 of them on any one device, and in every trip group one device is named exactly 12 times by each device of the group. Columns 1 and 2 of one device's triplets together name at most 2 wavevectors homed on any one device, and one device is named exactly 2 times by every device. Wavevectors may repeat.
All inputs are finite; a program needn't handle non-finite values.
Results may differ from the reference program's by a relative error of at most 0.0003.
Values may be sent and summed in bfloat16 or wider, within the bound.
No kernel may reach another device: no remote copies, remote signals or barrier semaphores. Data moves between devices by JAX's collectives and lax.ppermute only.
A program may use at most 128 MiB of HBM per device.

```python
import math
import jax
import jax.numpy as jnp
from jax import lax

NB = 64
COLS = 12
Q_DEV = 64
TRIP_DEV = 24
ITERS = 2
NQ = 2048
TRIPLET_TOTAL = 768
CAP0 = 12
N_TRIP = 8
N_ROW = 4


def draw_triplets(key, part):
    devices = N_TRIP * N_ROW
    full_owner = jax.random.randint(jax.random.fold_in(key, 11), (), 0, devices)
    heavy_rows = jax.random.randint(jax.random.fold_in(key, 12), (N_TRIP,), 0, N_ROW)

    def one_device(device):
        sub = jax.random.fold_in(jax.random.fold_in(key, 13), device)
        keys = jax.random.split(sub, 7)
        group_id = device // N_ROW
        heavy_row = heavy_rows[group_id]
        offsets = jax.random.randint(keys[0], (TRIP_DEV,), 1, N_ROW)
        position = jnp.arange(TRIP_DEV)
        target = jnp.where(position < CAP0, heavy_row, (heavy_row + offsets) % N_ROW)
        first = (group_id * N_ROW + target) * Q_DEV + jax.random.randint(keys[1], (TRIP_DEV,), 0, Q_DEV)
        first = first[jax.random.permutation(keys[2], TRIP_DEV)]
        visit_order = jax.random.permutation(keys[3], devices)
        where_full = jnp.argmax(visit_order == full_owner)
        leading = visit_order[0]
        visit_order = visit_order.at[where_full].set(leading).at[0].set(full_owner)
        request = jnp.arange(2 * TRIP_DEV)
        owner_dev = visit_order[request % devices]
        second = owner_dev * Q_DEV + jax.random.randint(keys[5], (2 * TRIP_DEV,), 0, Q_DEV)
        second = second[jax.random.permutation(keys[6], 2 * TRIP_DEV)].reshape(TRIP_DEV, 2)
        return jnp.concatenate([first[:, None], second], axis=1)
    listed = jax.vmap(one_device)(jnp.arange(devices))
    return listed.reshape(TRIP_DEV * devices, 3).astype(jnp.int32)


def touch_ends(result, key, low, high):
    place = [jax.random.randint(jax.random.fold_in(key, axis), (), 0, length) for axis, length in enumerate(result.shape)]
    main_axis = result.shape.index(max(result.shape))
    next_to = place[:main_axis] + [(place[main_axis] + 1) % result.shape[main_axis]] + place[main_axis + 1:]
    return result.at[tuple(place)].set(low).at[tuple(next_to)].set(high)


def shard_levels(rng, extent, cuts, low, high):
    factor_of = 1.0
    for dim, parts in cuts:
        draws = jax.random.uniform(jax.random.fold_in(jax.random.fold_in(rng, 6), dim), (parts,), jnp.float32, low / len(cuts), high / len(cuts))
        factor_of = factor_of * jnp.repeat(jnp.exp(draws), extent[dim] // parts).reshape((-1,) + (1,) * (len(extent) - 1 - dim))
    return factor_of


def noise(own_key, shape, spread, most, shards=(), kind=jnp.bfloat16):
    drawn = jax.random.normal(own_key, shape, jnp.float32) * spread
    if len(shards) > 0:
        drawn = shard_levels(own_key, shape, shards, -0.22, 0.18) * drawn
    return jnp.clip(drawn, min=-most, max=most).astype(kind)


def setup_inputs(seed: int = 0) -> dict:
    streams_of = jax.random.split(jax.random.key(seed), 8)
    return {
        "eigvecs": noise(streams_of[0], (NQ, NB, 2 * NB), (2 * NB) ** -0.5, 0.5, ((0, 32),)),
        "cubic": noise(streams_of[1], (TRIPLET_TOTAL, NB, NB * NB), (NB * NB) ** -0.5, 0.09375, ((0, 32),)),
        "triplets": draw_triplets(jax.random.fold_in(streams_of[7], 71), 0),
        "weights": touch_ends(jax.random.randint(streams_of[3], (TRIPLET_TOTAL,), 1, 7), jax.random.fold_in(streams_of[3], 1), 1, 6).astype(jnp.int32),
        "deviation": noise(streams_of[4], (NQ, NB * COLS), 1.0, 6.0, ((0, 32),), jnp.float32),
        "source": noise(streams_of[5], (NQ, NB * COLS), 1.0, 6.0, ((0, 32),), jnp.float32),
        "base_rate": jnp.clip(jnp.exp(math.log(2.0) - 1.3862944 * jax.random.uniform(streams_of[6], (NQ, NB), jnp.float32) ** shard_levels(streams_of[6], (NQ, NB), ((0, 32),), -0.2, 0.2)), 0.5, 2.0),
    }


damping = 0.7


def contract(tensor, vec_one, vec_two, vec_three, weight):
    branches = vec_one.shape[0]
    flat = tensor.reshape(branches * branches, branches)
    section_one = jnp.dot(flat, vec_three, preferred_element_type=jnp.float32).astype(jnp.bfloat16)
    section_one = section_one.reshape(branches, branches, 2 * branches)
    section_two = jnp.einsum('ijx,jy->ixy', section_one.astype(jnp.float32), vec_two.astype(jnp.float32))
    real_part = section_two[:, :branches, :branches] - section_two[:, branches:, branches:]
    imag_part = section_two[:, :branches, branches:] + section_two[:, branches:, :branches]
    mixed = jnp.stack([real_part, imag_part], 1).astype(jnp.bfloat16).reshape(branches, 2 * branches * branches)
    section_three = jnp.dot(vec_one.T, mixed, preferred_element_type=jnp.float32)
    section_three = section_three.reshape(2, branches, 2, branches, branches)
    vreal = section_three[0, :, 0] - section_three[1, :, 1]
    vimag = section_three[0, :, 1] + section_three[1, :, 0]
    power = (vreal * vreal + vimag * vimag) * weight.astype(jnp.float32)
    return jnp.sum(power, 1).astype(jnp.bfloat16), jnp.sum(power, 2).astype(jnp.bfloat16)


def reference(eigvecs, cubic, triplets, weights, deviation, source, base_rate):
    def one_triplet(bundle):
        tensor, listed, weight = bundle
        chosen = jnp.take(eigvecs, listed, axis=0)
        return contract(tensor, chosen[0], chosen[1], chosen[2], weight)

    first_pairing, second_pairing = lax.map(one_triplet, (cubic, triplets, weights))
    row_index = triplets[:, 0]
    rate_terms = jnp.sum(first_pairing.astype(jnp.float32), 2) + jnp.sum(second_pairing.astype(jnp.float32), 2)
    total_rate = base_rate + jax.ops.segment_sum(rate_terms, row_index, num_segments=NQ)
    phonon_state = deviation.reshape(NQ, NB, COLS)
    driven = source.reshape(NQ, NB, COLS)
    for update in range(ITERS):
        coupling_factors = jnp.einsum('hzy,hye->hze', first_pairing.astype(jnp.float32), jnp.take(phonon_state, triplets[:, 1], axis=0), precision=lax.Precision.HIGHEST)
        coupling_factors = coupling_factors + jnp.einsum('hzy,hye->hze', second_pairing.astype(jnp.float32), jnp.take(phonon_state, triplets[:, 2], axis=0), precision=lax.Precision.HIGHEST)
        coupled = jax.ops.segment_sum(coupling_factors, row_index, num_segments=NQ)
        phonon_state = (1.0 - damping) * phonon_state + damping * (driven + coupled) / total_rate[:, :, None]
    return phonon_state.reshape(NQ, NB * COLS)
```

```python
import functools

import jax
import jax.numpy as jnp
from jax import lax
from jax.experimental import pallas as pl
from jax.experimental.pallas import tpu as pltpu
from jax.sharding import PartitionSpec as P

ITERS = 2
DAMPING = 0.7
AXES = ("trip", "row")
F32 = jnp.float32
BF16 = jnp.bfloat16
CONTRACT_LANES = (((1,), (1,)), ((), ()))
MIB = 2**20


def ranks_of(target):
    extent = target.shape[0]
    matches = target[:, None] == target[None, :]
    earlier = lax.broadcasted_iota(jnp.int32, (extent, extent), 1) < lax.broadcasted_iota(
        jnp.int32, (extent, extent), 0
    )
    return jnp.sum((matches & earlier).astype(jnp.int32), axis=1)


def pack_ints(places, values, extent):
    onehot = lax.broadcasted_iota(jnp.int32, (extent, places.shape[0]), 0) == places[None, :]
    return jnp.sum(jnp.where(onehot, values[None, :], 0), axis=1)


def from_peers(blocks):
    count = len(blocks)
    return [blocks[0]] + [
        lax.ppermute(blocks[d], "row", [(i, (i + d) % count) for i in range(count)])
        for d in range(1, count)
    ]


def first_kernel(places, vec_ref, cubic_ref, out_ref):
    mixer = vec_ref[0].astype(F32).T.astype(BF16)
    extent = cubic_ref.shape[2]
    chunk = min(512, extent)
    for start in range(0, extent, chunk):
        part = cubic_ref[0, :, start : start + chunk]
        out_ref[0, :, start : start + chunk] = jnp.dot(
            mixer, part, preferred_element_type=F32
        ).astype(BF16)


def contract_first(places, table, cubic):
    count, branches, pairs = cubic.shape
    both = 2 * branches
    return pl.pallas_call(
        first_kernel,
        grid_spec=pltpu.PrefetchScalarGridSpec(
            num_scalar_prefetch=1,
            grid=(count,),
            in_specs=[
                pl.BlockSpec((1, branches, both), lambda t, places: (places[t], 0, 0)),
                pl.BlockSpec((1, branches, pairs), lambda t, places: (t, 0, 0)),
            ],
            out_specs=pl.BlockSpec((1, both, pairs), lambda t, places: (t, 0, 0)),
        ),
        out_shape=jax.ShapeDtypeStruct((count, both, pairs), BF16),
        compiler_params=pltpu.CompilerParams(vmem_limit_bytes=32 * MIB),
        cost_estimate=pl.CostEstimate(
            flops=2 * count * both * branches * pairs,
            bytes_accessed=2 * count * (both + branches) * pairs,
            transcendentals=0,
        ),
        name="contract_first",
    )(places, table, cubic)


def second_kernel(
    stride, second_place, third_place, weights, second_ref, third_ref, first_ref, pair_ref, turned
):
    branches = second_ref.shape[1]
    both = 2 * branches
    third = third_ref[0].astype(F32).T
    third_real, third_imag = third[:branches], third[branches:]
    none = jnp.zeros_like(third_real)
    third_mixer = jnp.concatenate(
        [
            jnp.concatenate([third_real, none, -third_imag, none], 1),
            jnp.concatenate([none, third_real, none, -third_imag], 1),
        ],
        0,
    ).astype(BF16)
    second = second_ref[0].astype(F32).T
    second_mixer = jnp.concatenate([second[:branches], second[branches:]], 1).astype(BF16)
    for group in range(branches // 4):
        rows = []
        for half in range(2):
            start = (2 * group + half) * both
            real = first_ref[0, :branches, start : start + both]
            imag = first_ref[0, branches:, start : start + both]
            rows += [jnp.concatenate([real, imag], 1), jnp.concatenate([imag, -real], 1)]
        mixed = lax.dot_general(
            third_mixer, jnp.concatenate(rows, 0), CONTRACT_LANES, preferred_element_type=F32
        )
        for half in range(2):
            for parity in range(2):
                turned[pl.ds(4 * group + 2 * half + parity, branches, stride=stride), :] = mixed[
                    parity * branches : (parity + 1) * branches, half * both : (half + 1) * both
                ]
    total = jnp.zeros((branches, both), F32)
    for group in range(branches // 2):
        columns = []
        for half in range(2):
            start = (2 * group + half) * stride
            block = turned[start : start + branches, :].astype(BF16)
            rotated = jnp.concatenate([-block[:, branches:], block[:, :branches]], 1)
            columns.append(jnp.concatenate([block, rotated], 0))
        values = jnp.dot(second_mixer, jnp.concatenate(columns, 1), preferred_element_type=F32)
        power = values * values
        total = total + power[:, :both] + power[:, both:]
        over_b = jnp.sum(power, 0, keepdims=True)
        turned[pl.ds(2 * group, 1), :] = over_b[:, :both]
        turned[pl.ds(2 * group + 1, 1), :] = over_b[:, both:]
    weight = weights[pl.program_id(0)].astype(F32)
    left = lax.broadcasted_iota(jnp.int32, (branches, both), 1) < branches
    for part, parted in enumerate((total, turned[:branches, :])):
        pairing = (parted + pltpu.roll(parted, branches, 1)) * weight
        pair_ref[0, part * both : part * both + branches, :] = jnp.where(
            left, pairing, 0.0
        ).astype(BF16)
        pair_ref[0, part * both + branches : (part + 1) * both, :] = jnp.where(
            left, 0.0, pairing
        ).astype(BF16)


def contract_rest(second_place, third_place, weights, table, first):
    count, both, pairs = first.shape
    branches = both // 2
    stride = branches + 8
    return pl.pallas_call(
        functools.partial(second_kernel, stride),
        grid_spec=pltpu.PrefetchScalarGridSpec(
            num_scalar_prefetch=3,
            grid=(count,),
            in_specs=[
                pl.BlockSpec((1, branches, both), lambda t, two, three, w: (two[t], 0, 0)),
                pl.BlockSpec((1, branches, both), lambda t, two, three, w: (three[t], 0, 0)),
                pl.BlockSpec((1, both, pairs), lambda t, two, three, w: (t, 0, 0)),
            ],
            out_specs=pl.BlockSpec((1, 2 * both, both), lambda t, two, three, w: (t, 0, 0)),
            scratch_shapes=[pltpu.VMEM((branches * stride, both), F32)],
        ),
        out_shape=jax.ShapeDtypeStruct((count, 2 * both, both), BF16),
        compiler_params=pltpu.CompilerParams(vmem_limit_bytes=32 * MIB),
        cost_estimate=pl.CostEstimate(
            flops=8 * count * both * branches * pairs,
            bytes_accessed=2 * count * both * pairs,
            transcendentals=0,
        ),
        name="contract_rest",
    )(second_place, third_place, weights, table, table, first)


def terms_kernel(
    columns, second_place, third_place, row_place, table_ref, pair_ref, *rest
):
    out_refs, packed = rest[:-1], rest[-1]
    rows, lanes = table_ref.shape[1:]
    packed[...] = jnp.zeros_like(packed)
    row = lax.broadcasted_iota(jnp.int32, (rows, lanes), 0)
    lane = lax.broadcasted_iota(jnp.int32, (rows, lanes), 1)
    is_rest = (row == columns - rows + 1) & (lane >= lanes // 2)
    for t in range(pair_ref.shape[0]):
        states = jnp.concatenate([table_ref[second_place[t]], table_ref[third_place[t]]], 1)
        terms = jnp.dot(states, pair_ref[t], preferred_element_type=F32)
        short = terms.astype(BF16).astype(F32)
        terms = jnp.where(is_rest, pltpu.roll(terms - short, 1, 0), terms)
        packed[row_place[t]] = terms.astype(BF16)
    cap = out_refs[0].shape[0]
    for d, out_ref in enumerate(out_refs):
        out_ref[...] = packed[d * cap : (d + 1) * cap]


def coupling_terms(second_place, third_place, row_place, table, pairs, columns, row_count, row_cap):
    rows, lanes = table.shape[1:]
    return pl.pallas_call(
        functools.partial(terms_kernel, columns),
        in_specs=[pl.BlockSpec(memory_space=pltpu.SMEM)] * 3
        + [pl.BlockSpec(memory_space=pltpu.VMEM)] * 2,
        out_specs=[pl.BlockSpec(memory_space=pltpu.VMEM)] * row_count,
        out_shape=[jax.ShapeDtypeStruct((row_cap, rows, lanes), BF16)] * row_count,
        scratch_shapes=[pltpu.VMEM((row_count * row_cap, rows, lanes), BF16)],
        compiler_params=pltpu.CompilerParams(vmem_limit_bytes=16 * MIB),
        name="coupling_terms",
    )(second_place, third_place, row_place, table, pairs)


def update_kernel(columns, first, last, codes, queries, *rest):
    row_count = codes.shape[0]
    arrived, rest = rest[:row_count], rest[row_count:]
    state_ref, source_ref, rate_ref = rest[:3]
    new_ref, next_ref, total = rest[3:]
    homes, rows, lanes = state_ref.shape
    total[...] = jnp.zeros_like(total)
    for d in range(row_count):
        for slot in range(codes.shape[1]):
            code = codes[d, slot]
            total[code] += arrived[d][slot].astype(F32)
    coupled = total[1:]
    if first:
        at = columns - rows
        rate = coupled[:, at : at + 1, :] + coupled[:, at + 1 : at + 2, :]
        lane = lax.broadcasted_iota(jnp.int32, rate.shape, 2)
        rate = jnp.where(lane < lanes // 2, pltpu.roll(rate, lanes // 2, 2), rate)
        rate = jnp.broadcast_to(rate + rate_ref[...], (homes, rows, lanes))
    else:
        rate = rate_ref[...]
    new = (1.0 - DAMPING) * state_ref[...] + DAMPING * (source_ref[...] + coupled) / rate
    new_ref[...] = new
    if first:
        next_ref[0][...] = rate
    if not last:
        send_ref = next_ref[-1]
        for slot in range(queries.shape[0]):
            send_ref[slot] = new_ref[queries[slot]].astype(BF16)


def update(codes, queries, arrived, state, source, rate, columns, first, last):
    homes, rows, lanes = state.shape
    outs = [jax.ShapeDtypeStruct(state.shape, F32)]
    if first:
        outs.append(jax.ShapeDtypeStruct(state.shape, F32))
    if not last:
        outs.append(jax.ShapeDtypeStruct((queries.shape[0], rows, lanes), BF16))
    row_count = len(arrived)

    def kernel(codes, queries, *refs):
        ins = refs[: row_count + 3]
        new_ref = refs[row_count + 3]
        more = refs[row_count + 4 : row_count + 3 + len(outs)]
        update_kernel(columns, first, last, codes, queries, *ins, new_ref, more, refs[-1])

    return pl.pallas_call(
        kernel,
        in_specs=[pl.BlockSpec(memory_space=pltpu.SMEM)] * 2
        + [pl.BlockSpec(memory_space=pltpu.VMEM)] * (row_count + 3),
        out_specs=[pl.BlockSpec(memory_space=pltpu.VMEM)] * len(outs),
        out_shape=outs,
        scratch_shapes=[pltpu.VMEM((homes + 1, rows, lanes), F32)],
        compiler_params=pltpu.CompilerParams(vmem_limit_bytes=16 * MIB),
        name="update",
    )(codes, queries, *arrived, state, source, rate)


def body(eigvecs, cubic, triplets, weights, deviation, source, base_rate):
    row_count = lax.axis_size("row")
    devices = lax.axis_size("trip") * row_count
    home_rows, branches = eigvecs.shape[:2]
    trip_local = cubic.shape[0]
    columns = deviation.shape[1] // branches
    far_cap = (2 * trip_local + devices - 1) // devices
    row_cap = trip_local // 2
    row_slots = row_count * row_cap
    rows = 8 * ((columns + 2 + 15) // 16)

    def packed(values):
        values = jnp.swapaxes(values.reshape(home_rows, branches, columns), 1, 2)
        values = jnp.pad(values, ((0, 0), (0, 2 * rows - columns), (0, 0)))
        values = values.reshape(home_rows, 2, rows, branches)
        return jnp.swapaxes(values, 1, 2).reshape(home_rows, rows, 2 * branches)

    def unpacked(values):
        values = jnp.swapaxes(values.reshape(home_rows, rows, 2, branches), 1, 2)
        values = values.reshape(home_rows, 2 * rows, branches)[:, :columns]
        return jnp.swapaxes(values, 1, 2).reshape(home_rows, branches * columns)

    first_dev = triplets[:, 0] // home_rows
    first_local = triplets[:, 0] - first_dev * home_rows
    ahead = (first_dev - lax.axis_index("row")) % row_count
    row_place = ahead * row_cap + ranks_of(ahead)
    row_codes = pack_ints(row_place, first_local + 1, row_slots).reshape(row_count, row_cap)
    codes = jnp.stack(from_peers([row_codes[d] for d in range(row_count)]))
    row_queries = jnp.maximum(codes - 1, 0)

    far_index = triplets[:, 1:].reshape(-1)
    far_owner = far_index // home_rows
    far_place = far_owner * far_cap + ranks_of(far_owner)
    far_queries = pack_ints(
        far_place, far_index - far_owner * home_rows, devices * far_cap
    ).reshape(devices, far_cap)

    def far(values):
        return lax.all_to_all(values, AXES, split_axis=0, concat_axis=0, tiled=True)

    queries = far(far_queries).reshape(-1)
    second_place, third_place = far_place.reshape(trip_local, 2).T

    far_table = far(jnp.take(eigvecs, queries, axis=0, mode="clip"))
    first_table = jnp.concatenate(
        [jnp.take(eigvecs, row_queries[0], axis=0, mode="clip")]
        + [
            lax.ppermute(
                jnp.take(eigvecs, row_queries[d], axis=0, mode="clip"),
                "row",
                [(i, (i - d) % row_count) for i in range(row_count)],
            )
            for d in range(1, row_count)
        ],
        0,
    )
    first_part = contract_first(row_place, first_table, cubic)

    state = packed(deviation)
    driven = packed(source)
    one = lax.broadcasted_iota(jnp.int32, state.shape[1:], 0) + rows * (
        lax.broadcasted_iota(jnp.int32, state.shape[1:], 1) // branches
    )
    sent = jnp.where(one == columns, 1.0, state).astype(BF16)
    arrived_state = far(jnp.take(sent, queries, axis=0, mode="clip"))
    rate = jnp.concatenate([base_rate, base_rate], 1)[:, None, :]

    pairs = contract_rest(second_place, third_place, weights, far_table, first_part)

    for step in range(ITERS):
        terms = coupling_terms(
            second_place, third_place, row_place, arrived_state, pairs, columns, row_count, row_cap
        )
        arrived = from_peers(terms)
        first, last = step == 0, step == ITERS - 1
        results = update(codes, queries, arrived, state, driven, rate, columns, first, last)
        state = results[0]
        if first:
            rate = results[1]
        if not last:
            arrived_state = far(results[-1])
    return unpacked(state)


def solution(mesh):
    whole = P(AXES, None, None)
    flat = P(AXES, None)
    in_specs = (whole, whole, flat, P(AXES), flat, flat, flat)
    return jax.shard_map(body, mesh=mesh, in_specs=in_specs, out_specs=flat, check_vma=False)
```

```python
import functools

import jax
import jax.numpy as jnp
from jax import lax
from jax.experimental import pallas as pl
from jax.experimental.pallas import tpu as pltpu
from jax.sharding import PartitionSpec as P

ITERS = 2
DAMPING = 0.7
AXES = ("trip", "row")
F32 = jnp.float32
BF16 = jnp.bfloat16
LANES = 128
MIB = 2**20


def ranks_of(target):
    extent = target.shape[0]
    matches = target[:, None] == target[None, :]
    earlier = lax.broadcasted_iota(jnp.int32, (extent, extent), 1) < lax.broadcasted_iota(
        jnp.int32, (extent, extent), 0
    )
    return jnp.sum((matches & earlier).astype(jnp.int32), axis=1)


def pack_ints(places, values, extent):
    onehot = lax.broadcasted_iota(jnp.int32, (extent, places.shape[0]), 0) == places[None, :]
    return jnp.sum(jnp.where(onehot, values[None, :], 0), axis=1)


def from_peers(blocks):
    count = len(blocks)
    return [blocks[0]] + [
        lax.ppermute(blocks[d], "row", [(i, (i + d) % count) for i in range(count)])
        for d in range(1, count)
    ]


def lookup_kernel(far_queries, row_queries, vec_ref, state_ref, far_ref, far_state_ref, *row_refs):
    for slot in range(far_queries.shape[0]):
        far_ref[slot] = vec_ref[far_queries[slot]]
        far_state_ref[slot] = state_ref[far_queries[slot]]
    for d, row_ref in enumerate(row_refs):
        for slot in range(row_ref.shape[0]):
            row_ref[slot] = vec_ref[row_queries[d, slot]]


def look_up(far_queries, row_queries, eigvecs, state):
    row_count, row_cap = row_queries.shape
    far_slots = far_queries.shape[0]
    outs = [
        jax.ShapeDtypeStruct((far_slots,) + eigvecs.shape[1:], eigvecs.dtype),
        jax.ShapeDtypeStruct((far_slots,) + state.shape[1:], state.dtype),
    ] + [jax.ShapeDtypeStruct((row_cap,) + eigvecs.shape[1:], eigvecs.dtype)] * row_count
    found = pl.pallas_call(
        lookup_kernel,
        in_specs=[pl.BlockSpec(memory_space=pltpu.SMEM)] * 2
        + [pl.BlockSpec(memory_space=pltpu.VMEM)] * 2,
        out_specs=[pl.BlockSpec(memory_space=pltpu.VMEM)] * len(outs),
        out_shape=outs,
        compiler_params=pltpu.CompilerParams(vmem_limit_bytes=16 * MIB),
        name="look_up",
    )(far_queries, row_queries, eigvecs, state)
    return found[0], found[1], found[2:]


def first_kernel(places, one_ref, two_ref, cubic_ref, out_ref):
    branches = cubic_ref.shape[1]
    both = 2 * branches
    one, two = one_ref[0], two_ref[0]
    none = jnp.zeros((branches, branches), one.dtype)
    mixer = jnp.concatenate(
        [
            jnp.concatenate([one[:, :branches], none, one[:, branches:], none], 1),
            jnp.concatenate([none, two[:, :branches], none, two[:, branches:]], 1),
        ],
        0,
    )
    step = 4
    for start in range(0, branches, step):
        lanes = slice(start * branches, (start + step) * branches)
        turned = jnp.concatenate([cubic_ref[0, :, lanes], cubic_ref[1, :, lanes]], 0).T
        mixed = jnp.dot(turned, mixer, preferred_element_type=F32).astype(BF16)
        for j in range(step):
            for part in range(2):
                out_ref[0, start + j, part * branches : (part + 1) * branches] = mixed[
                    j * branches : (j + 1) * branches, part * both : (part + 1) * both
                ]


def contract_first(places, table, cubic):
    count, branches, pairs = cubic.shape
    both = 2 * branches
    return pl.pallas_call(
        first_kernel,
        grid_spec=pltpu.PrefetchScalarGridSpec(
            num_scalar_prefetch=1,
            grid=(count // 2,),
            in_specs=[
                pl.BlockSpec((1, branches, both), lambda t, places: (places[2 * t], 0, 0)),
                pl.BlockSpec((1, branches, both), lambda t, places: (places[2 * t + 1], 0, 0)),
                pl.BlockSpec((2, branches, pairs), lambda t, places: (t, 0, 0)),
            ],
            out_specs=pl.BlockSpec((1, branches, both, both), lambda t, places: (t, 0, 0, 0)),
        ),
        out_shape=jax.ShapeDtypeStruct((count // 2, branches, both, both), BF16),
        compiler_params=pltpu.CompilerParams(vmem_limit_bytes=60 * MIB),
        cost_estimate=pl.CostEstimate(
            flops=2 * count * both * branches * pairs,
            bytes_accessed=2 * count * (both + branches) * pairs,
            transcendentals=0,
        ),
        name="contract_first",
    )(places, table, table, cubic)


def second_kernel(
    stride, second_place, third_place, weights, *refs
):
    second_refs, third_refs = refs[:2], refs[2:4]
    first_ref, pair_ref, turned = refs[4:]
    branches = second_refs[0].shape[1]
    both = 2 * branches

    def mixer(vec_refs):
        columns = []
        for vec_ref in vec_refs:
            vectors = vec_ref[0].astype(F32).T
            real, imag = vectors[:branches], vectors[branches:]
            columns += [jnp.concatenate([real, imag], 0), jnp.concatenate([-imag, real], 0)]
        return jnp.concatenate(columns, 1).astype(BF16)

    left = lax.broadcasted_iota(jnp.int32, (both, both), 1) < branches
    none = jnp.zeros((both, both), BF16)

    def apart(block):
        return jnp.concatenate([jnp.where(left, block, none), jnp.where(left, none, block)], 0)

    second_mixer, third_mixer = mixer(second_refs), mixer(third_refs)
    for j in range(0, branches, 2):
        mixed = jnp.dot(
            third_mixer,
            jnp.concatenate([apart(first_ref[0, j]), apart(first_ref[0, j + 1])], 1),
            preferred_element_type=F32,
        )
        for half in range(2):
            for part in range(2):
                turned[pl.ds(part * branches + j + half, branches, stride=stride), :] = mixed[
                    part * branches : (part + 1) * branches, half * both : (half + 1) * both
                ]
    total = jnp.zeros((branches, both), F32)
    for c in range(0, branches, 2):
        columns = [
            apart(turned[(c + half) * stride : (c + half) * stride + both, :].astype(BF16))
            for half in range(2)
        ]
        values = jnp.dot(second_mixer, jnp.concatenate(columns, 1), preferred_element_type=F32)
        real, imag = values[:branches], values[branches:]
        power = real * real + imag * imag
        over_b = jnp.sum(power, 0, keepdims=True)
        for half in range(2):
            lanes = slice(half * both, (half + 1) * both)
            total = total + power[:, lanes]
            turned[pl.ds(c + half, 1), :] = over_b[:, lanes]
    step = pl.program_id(0)
    left = left[:branches]
    weight = jnp.where(left, weights[2 * step].astype(F32), weights[2 * step + 1].astype(F32))
    for part, parted in enumerate((total, turned[:branches, :])):
        own = parted * weight
        other = pltpu.roll(own, branches, 1)
        for t, (upper, lower) in enumerate(((own, other), (other, own))):
            start = part * both
            pair_ref[t, start : start + branches, :] = jnp.where(left, upper, 0.0).astype(BF16)
            pair_ref[t, start + branches : start + both, :] = jnp.where(left, 0.0, lower).astype(
                BF16
            )


def contract_rest(second_place, third_place, weights, table, first):
    steps, branches, both = first.shape[:3]
    stride = both + 8

    def vectors(which, t):
        return pl.BlockSpec(
            (1, branches, both), lambda s, *places: (places[which][2 * s + t], 0, 0)
        )

    return pl.pallas_call(
        functools.partial(second_kernel, stride),
        grid_spec=pltpu.PrefetchScalarGridSpec(
            num_scalar_prefetch=3,
            grid=(steps,),
            in_specs=[vectors(0, 0), vectors(0, 1), vectors(1, 0), vectors(1, 1)]
            + [pl.BlockSpec((1, branches, both, both), lambda s, *places: (s, 0, 0, 0))],
            out_specs=pl.BlockSpec((2, 2 * both, both), lambda s, *places: (s, 0, 0)),
            scratch_shapes=[pltpu.VMEM((branches * stride, both), F32)],
        ),
        out_shape=jax.ShapeDtypeStruct((2 * steps, 2 * both, both), BF16),
        compiler_params=pltpu.CompilerParams(vmem_limit_bytes=60 * MIB),
        cost_estimate=pl.CostEstimate(
            flops=16 * steps * both * both * branches * branches,
            bytes_accessed=2 * steps * both * both * branches,
            transcendentals=0,
        ),
        name="contract_rest",
    )(second_place, third_place, weights, table, table, table, table, first)


def terms_kernel(
    columns, second_place, third_place, row_place, table_ref, pair_ref, *rest
):
    out_refs, packed = rest[:-1], rest[-1]
    rows, lanes = table_ref.shape[1:]
    packed[...] = jnp.zeros_like(packed)
    row = lax.broadcasted_iota(jnp.int32, (rows, lanes), 0)
    lane = lax.broadcasted_iota(jnp.int32, (rows, lanes), 1)
    is_rest = (row == columns - rows + 1) & (lane >= lanes // 2)
    for t in range(pair_ref.shape[0]):
        states = jnp.concatenate([table_ref[second_place[t]], table_ref[third_place[t]]], 1)
        terms = jnp.dot(states, pair_ref[t], preferred_element_type=F32)
        short = terms.astype(BF16).astype(F32)
        terms = jnp.where(is_rest, pltpu.roll(terms - short, 1, 0), terms)
        packed[row_place[t]] = terms.astype(BF16)
    cap = out_refs[0].shape[0]
    for d, out_ref in enumerate(out_refs):
        out_ref[...] = packed[d * cap : (d + 1) * cap]


def coupling_terms(second_place, third_place, row_place, table, pairs, columns, row_count, row_cap):
    rows, lanes = table.shape[1:]
    return pl.pallas_call(
        functools.partial(terms_kernel, columns),
        in_specs=[pl.BlockSpec(memory_space=pltpu.SMEM)] * 3
        + [pl.BlockSpec(memory_space=pltpu.VMEM)] * 2,
        out_specs=[pl.BlockSpec(memory_space=pltpu.VMEM)] * row_count,
        out_shape=[jax.ShapeDtypeStruct((row_cap, rows, lanes), BF16)] * row_count,
        scratch_shapes=[pltpu.VMEM((row_count * row_cap, rows, lanes), BF16)],
        compiler_params=pltpu.CompilerParams(vmem_limit_bytes=16 * MIB),
        name="coupling_terms",
    )(second_place, third_place, row_place, table, pairs)


def update_kernel(columns, first, last, codes, queries, *rest):
    row_count = codes.shape[0]
    arrived, rest = rest[:row_count], rest[row_count:]
    state_ref, source_ref, rate_ref = rest[:3]
    new_ref, next_ref, total = rest[3:]
    homes, rows, lanes = state_ref.shape
    total[...] = jnp.zeros_like(total)
    for d in range(row_count):
        for slot in range(codes.shape[1]):
            code = codes[d, slot]
            total[code] += arrived[d][slot].astype(F32)
    coupled = total[1:]
    if first:
        at = columns - rows
        rate = coupled[:, at : at + 1, :] + coupled[:, at + 1 : at + 2, :]
        lane = lax.broadcasted_iota(jnp.int32, rate.shape, 2)
        rate = jnp.where(lane < lanes // 2, pltpu.roll(rate, lanes // 2, 2), rate)
        rate = jnp.broadcast_to(rate + rate_ref[...], (homes, rows, lanes))
    else:
        rate = rate_ref[...]
    new = (1.0 - DAMPING) * state_ref[...] + DAMPING * (source_ref[...] + coupled) / rate
    new_ref[...] = new
    if first:
        next_ref[0][...] = rate
    if not last:
        send_ref = next_ref[-1]
        for slot in range(queries.shape[0]):
            send_ref[slot] = new_ref[queries[slot]].astype(BF16)


def update(codes, queries, arrived, state, source, rate, columns, first, last):
    homes, rows, lanes = state.shape
    outs = [jax.ShapeDtypeStruct(state.shape, F32)]
    if first:
        outs.append(jax.ShapeDtypeStruct(state.shape, F32))
    if not last:
        outs.append(jax.ShapeDtypeStruct((queries.shape[0], rows, lanes), BF16))
    row_count = len(arrived)

    def kernel(codes, queries, *refs):
        ins = refs[: row_count + 3]
        new_ref = refs[row_count + 3]
        more = refs[row_count + 4 : row_count + 3 + len(outs)]
        update_kernel(columns, first, last, codes, queries, *ins, new_ref, more, refs[-1])

    return pl.pallas_call(
        kernel,
        in_specs=[pl.BlockSpec(memory_space=pltpu.SMEM)] * 2
        + [pl.BlockSpec(memory_space=pltpu.VMEM)] * (row_count + 3),
        out_specs=[pl.BlockSpec(memory_space=pltpu.VMEM)] * len(outs),
        out_shape=outs,
        scratch_shapes=[pltpu.VMEM((homes + 1, rows, lanes), F32)],
        compiler_params=pltpu.CompilerParams(vmem_limit_bytes=16 * MIB),
        name="update",
    )(codes, queries, *arrived, state, source, rate)


def body(eigvecs, cubic, triplets, weights, deviation, source, base_rate):
    row_count = lax.axis_size("row")
    devices = lax.axis_size("trip") * row_count
    home_rows, branches = eigvecs.shape[:2]
    trip_local = cubic.shape[0]
    columns = deviation.shape[1] // branches
    far_cap = (2 * trip_local + devices - 1) // devices
    row_cap = trip_local // 2
    row_slots = row_count * row_cap
    rows = 8 * ((columns + 2 + 15) // 16)

    def packed(values):
        values = jnp.swapaxes(values.reshape(home_rows, branches, columns), 1, 2)
        values = jnp.pad(values, ((0, 0), (0, 2 * rows - columns), (0, 0)))
        values = values.reshape(home_rows, 2, rows, branches)
        return jnp.swapaxes(values, 1, 2).reshape(home_rows, rows, 2 * branches)

    def unpacked(values):
        values = jnp.swapaxes(values.reshape(home_rows, rows, 2, branches), 1, 2)
        values = values.reshape(home_rows, 2 * rows, branches)[:, :columns]
        return jnp.swapaxes(values, 1, 2).reshape(home_rows, branches * columns)

    me = lax.axis_index("trip") * row_count + lax.axis_index("row")
    owner = triplets // home_rows
    local = triplets - owner * home_rows
    first_dev, far_owner = owner[:, 0], owner[:, 1:].reshape(-1)
    ahead = (first_dev - me) % row_count
    row_rank = ranks_of(first_dev)
    far_rank = ranks_of(far_owner)
    row_place = ahead * row_cap + row_rank
    far_place = far_owner * far_cap + far_rank
    message = pack_ints(
        jnp.concatenate([far_owner * LANES + far_rank, first_dev * LANES + far_cap + row_rank]),
        jnp.concatenate([local[:, 1:].reshape(-1), local[:, 0] + 1]),
        devices * LANES,
    ).reshape(devices, 1, LANES)

    def far(values):
        return lax.all_to_all(values, AXES, split_axis=0, concat_axis=0, tiled=True)

    heard = far(message)[:, 0]
    queries = heard[:, :far_cap].reshape(-1)
    second_place, third_place = far_place.reshape(trip_local, 2).T
    group = lax.dynamic_slice(
        heard, (lax.axis_index("trip") * row_count, far_cap), (row_count, row_cap)
    )
    codes = jnp.take(
        group, (lax.axis_index("row") - jnp.arange(row_count)) % row_count, axis=0, mode="clip"
    )

    state = packed(deviation)
    one = lax.broadcasted_iota(jnp.int32, state.shape[1:], 0) + rows * (
        lax.broadcasted_iota(jnp.int32, state.shape[1:], 1) // branches
    )
    sent_state = jnp.where(one == columns, 1.0, state).astype(BF16)
    far_vecs, far_state, row_vecs = look_up(queries, jnp.maximum(codes - 1, 0), eigvecs, sent_state)
    far_table = far(far_vecs)
    first_table = jnp.concatenate(
        [row_vecs[0]]
        + [
            lax.ppermute(row_vecs[d], "row", [(i, (i - d) % row_count) for i in range(row_count)])
            for d in range(1, row_count)
        ],
        0,
    )
    driven = packed(source)
    rate = jnp.concatenate([base_rate, base_rate], 1)[:, None, :]
    first_table, driven, rate = lax.optimization_barrier((first_table, driven, rate))
    first_part = contract_first(row_place, first_table, cubic)
    arrived_state = far(far_state)
    pairs = contract_rest(second_place, third_place, weights, far_table, first_part)

    for step in range(ITERS):
        terms = coupling_terms(
            second_place, third_place, row_place, arrived_state, pairs, columns, row_count, row_cap
        )
        arrived = from_peers(terms)
        first, last = step == 0, step == ITERS - 1
        results = update(codes, queries, arrived, state, driven, rate, columns, first, last)
        state = results[0]
        if first:
            rate = results[1]
        if not last:
            arrived_state = far(results[-1])
    return unpacked(state)


def solution(mesh):
    whole = P(AXES, None, None)
    flat = P(AXES, None)
    in_specs = (whole, whole, flat, P(AXES), flat, flat, flat)
    return jax.shard_map(body, mesh=mesh, in_specs=in_specs, out_specs=flat, check_vma=False)
```

```python
import functools

import jax
import jax.numpy as jnp
from jax import lax
from jax.experimental import pallas as pl
from jax.experimental.pallas import tpu as pltpu
from jax.sharding import PartitionSpec as P

ITERS = 2
DAMPING = 0.7
AXES = ("trip", "row")
F32 = jnp.float32
BF16 = jnp.bfloat16
LANES = 128
MIB = 2**20


def ranks_of(target):
    extent = target.shape[0]
    matches = target[:, None] == target[None, :]
    earlier = lax.broadcasted_iota(jnp.int32, (extent, extent), 1) < lax.broadcasted_iota(
        jnp.int32, (extent, extent), 0
    )
    return jnp.sum((matches & earlier).astype(jnp.int32), axis=1)


def pack_ints(places, values, extent):
    onehot = lax.broadcasted_iota(jnp.int32, (extent, places.shape[0]), 0) == places[None, :]
    return jnp.sum(jnp.where(onehot, values[None, :], 0), axis=1)


def from_peers(blocks):
    count = len(blocks)
    return [blocks[0]] + [
        lax.ppermute(blocks[d], "row", [(i, (i + d) % count) for i in range(count)])
        for d in range(1, count)
    ]


def lookup_kernel(queries, table_ref, *found_refs):
    cap = found_refs[0].shape[0]
    for d, found_ref in enumerate(found_refs):
        for slot in range(cap):
            found_ref[slot] = table_ref[queries[d * cap + slot]]


def look_up(queries, table, parts):
    cap = queries.shape[0] // parts
    return pl.pallas_call(
        lookup_kernel,
        in_specs=[
            pl.BlockSpec(memory_space=pltpu.SMEM),
            pl.BlockSpec(memory_space=pltpu.VMEM),
        ],
        out_specs=[pl.BlockSpec(memory_space=pltpu.VMEM)] * parts,
        out_shape=[jax.ShapeDtypeStruct((cap,) + table.shape[1:], table.dtype)] * parts,
        compiler_params=pltpu.CompilerParams(vmem_limit_bytes=16 * MIB),
        name="look_up",
    )(queries, table)


def first_kernel(places, one_ref, two_ref, cubic_ref, out_ref):
    branches = cubic_ref.shape[1]
    both = 2 * branches
    one, two = one_ref[0], two_ref[0]
    none = jnp.zeros((branches, branches), one.dtype)
    mixer = jnp.concatenate(
        [
            jnp.concatenate([one[:, :branches], none, one[:, branches:], none], 1),
            jnp.concatenate([none, two[:, :branches], none, two[:, branches:]], 1),
        ],
        0,
    )
    step = 4
    for start in range(0, branches, step):
        lanes = slice(start * branches, (start + step) * branches)
        turned = jnp.concatenate([cubic_ref[0, :, lanes], cubic_ref[1, :, lanes]], 0).T
        mixed = jnp.dot(turned, mixer, preferred_element_type=F32).astype(BF16)
        for j in range(step):
            for part in range(2):
                out_ref[0, start + j, part * branches : (part + 1) * branches] = mixed[
                    j * branches : (j + 1) * branches, part * both : (part + 1) * both
                ]


def contract_first(places, table, cubic):
    count, branches, pairs = cubic.shape
    both = 2 * branches
    return pl.pallas_call(
        first_kernel,
        grid_spec=pltpu.PrefetchScalarGridSpec(
            num_scalar_prefetch=1,
            grid=(count // 2,),
            in_specs=[
                pl.BlockSpec((1, branches, both), lambda t, places: (places[2 * t], 0, 0)),
                pl.BlockSpec((1, branches, both), lambda t, places: (places[2 * t + 1], 0, 0)),
                pl.BlockSpec((2, branches, pairs), lambda t, places: (t, 0, 0)),
            ],
            out_specs=pl.BlockSpec((1, branches, both, both), lambda t, places: (t, 0, 0, 0)),
        ),
        out_shape=jax.ShapeDtypeStruct((count // 2, branches, both, both), BF16),
        compiler_params=pltpu.CompilerParams(vmem_limit_bytes=60 * MIB),
        cost_estimate=pl.CostEstimate(
            flops=2 * count * both * branches * pairs,
            bytes_accessed=2 * count * (both + branches) * pairs,
            transcendentals=0,
        ),
        name="contract_first",
    )(places, table, table, cubic)


def second_kernel(stride, group, second_place, third_place, weights, *refs):
    second_refs, third_refs = refs[: 2 * group], refs[2 * group : 4 * group]
    first_ref, pair_ref, *scratch = refs[4 * group :]
    branches = first_ref.shape[1]
    both = 2 * branches

    def mixer(vec_refs):
        columns = []
        for vec_ref in vec_refs:
            vectors = vec_ref[0].astype(F32).T
            real, imag = vectors[:branches], vectors[branches:]
            columns += [jnp.concatenate([real, imag], 0), jnp.concatenate([-imag, real], 0)]
        return jnp.concatenate(columns, 1).astype(BF16)

    left = lax.broadcasted_iota(jnp.int32, (both, both), 1) < branches
    none = jnp.zeros((both, both), BF16)

    def apart(block):
        return jnp.concatenate([jnp.where(left, block, none), jnp.where(left, none, block)], 0)

    def over_k(pair, third_mixer, j):
        turned = scratch[pair % 2]
        mixed = jnp.dot(
            third_mixer,
            jnp.concatenate([apart(first_ref[pair, j]), apart(first_ref[pair, j + 1])], 1),
            preferred_element_type=F32,
        )
        for half in range(2):
            for part in range(2):
                turned[pl.ds(part * branches + j + half, branches, stride=stride), :] = mixed[
                    part * branches : (part + 1) * branches, half * both : (half + 1) * both
                ]

    def over_j(pair, second_mixer, c, total):
        turned = scratch[pair % 2]
        columns = [
            apart(turned[(c + half) * stride : (c + half) * stride + both, :].astype(BF16))
            for half in range(2)
        ]
        values = jnp.dot(second_mixer, jnp.concatenate(columns, 1), preferred_element_type=F32)
        real, imag = values[:branches], values[branches:]
        power = real * real + imag * imag
        over_b = jnp.sum(power, 0, keepdims=True)
        for half in range(2):
            lanes = slice(half * both, (half + 1) * both)
            total = total + power[:, lanes]
            turned[pl.ds(c + half, 1), :] = over_b[:, lanes]
        return total

    def finish(pair, total):
        first = 2 * (group * pl.program_id(0) + pair)
        near = left[:branches]
        weight = jnp.where(near, weights[first].astype(F32), weights[first + 1].astype(F32))
        for part, parted in enumerate((total, scratch[pair % 2][:branches, :])):
            own = parted * weight
            other = pltpu.roll(own, branches, 1)
            start = part * both
            for t, (upper, lower) in enumerate(((own, other), (other, own))):
                pair_ref[2 * pair + t, start : start + branches, :] = jnp.where(
                    near, upper, 0.0
                ).astype(BF16)
                pair_ref[2 * pair + t, start + branches : start + both, :] = jnp.where(
                    near, 0.0, lower
                ).astype(BF16)

    for phase in range(group + 1):
        before = phase - 1
        if phase < group:
            third_mixer = mixer(third_refs[2 * phase : 2 * phase + 2])
        if phase > 0:
            second_mixer = mixer(second_refs[2 * before : 2 * before + 2])
            total = jnp.zeros((branches, both), F32)
        for at in range(0, branches, 2):
            if phase > 0:
                total = over_j(before, second_mixer, at, total)
            if phase < group:
                over_k(phase, third_mixer, at)
        if phase > 0:
            finish(before, total)


def contract_rest(second_place, third_place, weights, table, first):
    pairs, branches, both = first.shape[:3]
    group = 2 if pairs % 2 == 0 else 1
    stride = both + 9

    def vectors(which, t):
        return pl.BlockSpec(
            (1, branches, both), lambda s, *places: (places[which][2 * group * s + t], 0, 0)
        )

    return pl.pallas_call(
        functools.partial(second_kernel, stride, group),
        grid_spec=pltpu.PrefetchScalarGridSpec(
            num_scalar_prefetch=3,
            grid=(pairs // group,),
            in_specs=[vectors(which, t) for which in range(2) for t in range(2 * group)]
            + [pl.BlockSpec((group, branches, both, both), lambda s, *places: (s, 0, 0, 0))],
            out_specs=pl.BlockSpec((2 * group, 2 * both, both), lambda s, *places: (s, 0, 0)),
            scratch_shapes=[pltpu.VMEM((branches * stride, both), F32)] * 2,
        ),
        out_shape=jax.ShapeDtypeStruct((2 * pairs, 2 * both, both), BF16),
        compiler_params=pltpu.CompilerParams(vmem_limit_bytes=32 * MIB),
        cost_estimate=pl.CostEstimate(
            flops=16 * pairs * both * both * branches * branches,
            bytes_accessed=2 * pairs * both * both * branches,
            transcendentals=0,
        ),
        name="contract_rest",
    )(second_place, third_place, weights, *[table] * (4 * group), first)


def terms_kernel(
    columns, second_place, third_place, row_place, table_ref, pair_ref, *rest
):
    out_refs, packed = rest[:-1], rest[-1]
    rows, lanes = table_ref.shape[1:]
    packed[...] = jnp.zeros_like(packed)
    row = lax.broadcasted_iota(jnp.int32, (rows, lanes), 0)
    lane = lax.broadcasted_iota(jnp.int32, (rows, lanes), 1)
    is_rest = (row == columns - rows + 1) & (lane >= lanes // 2)
    for t in range(pair_ref.shape[0]):
        states = jnp.concatenate([table_ref[second_place[t]], table_ref[third_place[t]]], 1)
        terms = jnp.dot(states, pair_ref[t], preferred_element_type=F32)
        short = terms.astype(BF16).astype(F32)
        terms = jnp.where(is_rest, pltpu.roll(terms - short, 1, 0), terms)
        packed[row_place[t]] = terms.astype(BF16)
    cap = out_refs[0].shape[0]
    for d, out_ref in enumerate(out_refs):
        out_ref[...] = packed[d * cap : (d + 1) * cap]


def coupling_terms(second_place, third_place, row_place, table, pairs, columns, row_count, row_cap):
    rows, lanes = table.shape[1:]
    return pl.pallas_call(
        functools.partial(terms_kernel, columns),
        in_specs=[pl.BlockSpec(memory_space=pltpu.SMEM)] * 3
        + [pl.BlockSpec(memory_space=pltpu.VMEM)] * 2,
        out_specs=[pl.BlockSpec(memory_space=pltpu.VMEM)] * row_count,
        out_shape=[jax.ShapeDtypeStruct((row_cap, rows, lanes), BF16)] * row_count,
        scratch_shapes=[pltpu.VMEM((row_count * row_cap, rows, lanes), BF16)],
        compiler_params=pltpu.CompilerParams(vmem_limit_bytes=16 * MIB),
        name="coupling_terms",
    )(second_place, third_place, row_place, table, pairs)


def update_kernel(columns, first, last, codes, queries, *rest):
    row_count = codes.shape[0]
    arrived, rest = rest[:row_count], rest[row_count:]
    state_ref, source_ref, rate_ref = rest[:3]
    new_ref, next_ref, total = rest[3:]
    homes, rows, lanes = state_ref.shape
    total[...] = jnp.zeros_like(total)
    for d in range(row_count):
        for slot in range(codes.shape[1]):
            code = codes[d, slot]
            total[code] += arrived[d][slot].astype(F32)
    coupled = total[1:]
    if first:
        at = columns - rows
        rate = coupled[:, at : at + 1, :] + coupled[:, at + 1 : at + 2, :]
        lane = lax.broadcasted_iota(jnp.int32, rate.shape, 2)
        rate = jnp.where(lane < lanes // 2, pltpu.roll(rate, lanes // 2, 2), rate)
        rate = jnp.broadcast_to(rate + rate_ref[...], (homes, rows, lanes))
    else:
        rate = rate_ref[...]
    new = (1.0 - DAMPING) * state_ref[...] + DAMPING * (source_ref[...] + coupled) / rate
    new_ref[...] = new
    if first:
        next_ref[0][...] = rate
    if not last:
        send_ref = next_ref[-1]
        for slot in range(queries.shape[0]):
            send_ref[slot] = new_ref[queries[slot]].astype(BF16)


def update(codes, queries, arrived, state, source, rate, columns, first, last):
    homes, rows, lanes = state.shape
    outs = [jax.ShapeDtypeStruct(state.shape, F32)]
    if first:
        outs.append(jax.ShapeDtypeStruct(state.shape, F32))
    if not last:
        outs.append(jax.ShapeDtypeStruct((queries.shape[0], rows, lanes), BF16))
    row_count = len(arrived)

    def kernel(codes, queries, *refs):
        ins = refs[: row_count + 3]
        new_ref = refs[row_count + 3]
        more = refs[row_count + 4 : row_count + 3 + len(outs)]
        update_kernel(columns, first, last, codes, queries, *ins, new_ref, more, refs[-1])

    return pl.pallas_call(
        kernel,
        in_specs=[pl.BlockSpec(memory_space=pltpu.SMEM)] * 2
        + [pl.BlockSpec(memory_space=pltpu.VMEM)] * (row_count + 3),
        out_specs=[pl.BlockSpec(memory_space=pltpu.VMEM)] * len(outs),
        out_shape=outs,
        scratch_shapes=[pltpu.VMEM((homes + 1, rows, lanes), F32)],
        compiler_params=pltpu.CompilerParams(vmem_limit_bytes=16 * MIB),
        name="update",
    )(codes, queries, *arrived, state, source, rate)


def body(eigvecs, cubic, triplets, weights, deviation, source, base_rate):
    row_count = lax.axis_size("row")
    devices = lax.axis_size("trip") * row_count
    home_rows, branches = eigvecs.shape[:2]
    trip_local = cubic.shape[0]
    columns = deviation.shape[1] // branches
    far_cap = (2 * trip_local + devices - 1) // devices
    row_cap = trip_local // 2
    row_slots = row_count * row_cap
    rows = 8 * ((columns + 2 + 15) // 16)

    def packed(values):
        values = jnp.swapaxes(values.reshape(home_rows, branches, columns), 1, 2)
        values = jnp.pad(values, ((0, 0), (0, 2 * rows - columns), (0, 0)))
        values = values.reshape(home_rows, 2, rows, branches)
        return jnp.swapaxes(values, 1, 2).reshape(home_rows, rows, 2 * branches)

    def unpacked(values):
        values = jnp.swapaxes(values.reshape(home_rows, rows, 2, branches), 1, 2)
        values = values.reshape(home_rows, 2 * rows, branches)[:, :columns]
        return jnp.swapaxes(values, 1, 2).reshape(home_rows, branches * columns)

    first_dev = triplets[:, 0] // home_rows
    first_local = triplets[:, 0] - first_dev * home_rows
    ahead = (first_dev - lax.axis_index("row")) % row_count
    row_place = ahead * row_cap + ranks_of(ahead)
    row_codes = pack_ints(row_place, first_local + 1, row_slots).reshape(row_count, row_cap)

    far_index = triplets[:, 1:].reshape(-1)
    far_owner = far_index // home_rows
    far_rank = ranks_of(far_owner)
    far_place = far_owner * far_cap + far_rank
    message = pack_ints(
        far_owner * LANES + far_rank, far_index - far_owner * home_rows, devices * LANES
    ).reshape(devices, 1, LANES)

    def far(values):
        return lax.all_to_all(values, AXES, split_axis=0, concat_axis=0, tiled=True)

    queries = far(message)[:, 0, :far_cap].reshape(-1)
    second_place, third_place = far_place.reshape(trip_local, 2).T
    codes = jnp.stack(from_peers([row_codes[d] for d in range(row_count)]))
    row_vecs = look_up(jnp.maximum(codes - 1, 0).reshape(-1), eigvecs, row_count)
    first_table = jnp.concatenate(
        [row_vecs[0]]
        + [
            lax.ppermute(row_vecs[d], "row", [(i, (i - d) % row_count) for i in range(row_count)])
            for d in range(1, row_count)
        ],
        0,
    )

    state = packed(deviation)
    one = lax.broadcasted_iota(jnp.int32, state.shape[1:], 0) + rows * (
        lax.broadcasted_iota(jnp.int32, state.shape[1:], 1) // branches
    )
    sent_state = jnp.where(one == columns, 1.0, state).astype(BF16)
    records = jnp.concatenate([eigvecs, sent_state], 1)
    queries, row_vecs = lax.optimization_barrier((queries, row_vecs))
    far_table = far(look_up(queries, records, 1)[0])
    driven = packed(source)
    rate = jnp.concatenate([base_rate, base_rate], 1)[:, None, :]
    first_table, driven, rate = lax.optimization_barrier((first_table, driven, rate))
    first_part = contract_first(row_place, first_table, cubic)
    arrived_state = far_table[:, branches:]
    pairs = contract_rest(second_place, third_place, weights, far_table, first_part)

    for step in range(ITERS):
        terms = coupling_terms(
            second_place, third_place, row_place, arrived_state, pairs, columns, row_count, row_cap
        )
        arrived = from_peers(terms)
        first, last = step == 0, step == ITERS - 1
        results = update(codes, queries, arrived, state, driven, rate, columns, first, last)
        state = results[0]
        if first:
            rate = results[1]
        if not last:
            arrived_state = far(results[-1])
    return unpacked(state)


def solution(mesh):
    whole = P(AXES, None, None)
    flat = P(AXES, None)
    in_specs = (whole, whole, flat, P(AXES), flat, flat, flat)
    return jax.shard_map(body, mesh=mesh, in_specs=in_specs, out_specs=flat, check_vma=False)
```

```python
import functools

import jax
import jax.numpy as jnp
from jax import lax
from jax.experimental import pallas as pl
from jax.experimental.pallas import tpu as pltpu
from jax.sharding import PartitionSpec as P

ITERS = 2
DAMPING = 0.7
AXES = ("trip", "row")
F32 = jnp.float32
BF16 = jnp.bfloat16
LANES = 128
MIB = 2**20


def ranks_of(target):
    extent = target.shape[0]
    matches = target[:, None] == target[None, :]
    earlier = lax.broadcasted_iota(jnp.int32, (extent, extent), 1) < lax.broadcasted_iota(
        jnp.int32, (extent, extent), 0
    )
    return jnp.sum((matches & earlier).astype(jnp.int32), axis=1)


def pack_ints(places, values, extent):
    onehot = lax.broadcasted_iota(jnp.int32, (extent, places.shape[0]), 0) == places[None, :]
    return jnp.sum(jnp.where(onehot, values[None, :], 0), axis=1)


def from_peers(blocks):
    count = len(blocks)
    return [blocks[0]] + [
        lax.ppermute(blocks[d], "row", [(i, (i + d) % count) for i in range(count)])
        for d in range(1, count)
    ]


def lookup_kernel(queries, table_ref, *found_refs):
    cap = found_refs[0].shape[0]
    for d, found_ref in enumerate(found_refs):
        for slot in range(cap):
            found_ref[slot] = table_ref[queries[d * cap + slot]]


def look_up(queries, table, parts):
    cap = queries.shape[0] // parts
    return pl.pallas_call(
        lookup_kernel,
        in_specs=[
            pl.BlockSpec(memory_space=pltpu.SMEM),
            pl.BlockSpec(memory_space=pltpu.VMEM),
        ],
        out_specs=[pl.BlockSpec(memory_space=pltpu.VMEM)] * parts,
        out_shape=[jax.ShapeDtypeStruct((cap,) + table.shape[1:], table.dtype)] * parts,
        compiler_params=pltpu.CompilerParams(vmem_limit_bytes=16 * MIB),
        name="look_up",
    )(queries, table)


def first_kernel(places, one_ref, two_ref, cubic_ref, out_ref):
    branches = cubic_ref.shape[1]
    both = 2 * branches
    one, two = one_ref[0], two_ref[0]
    none = jnp.zeros((branches, branches), one.dtype)
    mixer = jnp.concatenate(
        [
            jnp.concatenate([one[:, :branches], none, one[:, branches:], none], 1),
            jnp.concatenate([none, two[:, :branches], none, two[:, branches:]], 1),
        ],
        0,
    )
    step = 4
    for start in range(0, branches, step):
        lanes = slice(start * branches, (start + step) * branches)
        turned = jnp.concatenate([cubic_ref[0, :, lanes], cubic_ref[1, :, lanes]], 0).T
        mixed = jnp.dot(turned, mixer, preferred_element_type=F32).astype(BF16)
        for j in range(step):
            for part in range(2):
                out_ref[0, start + j, part * branches : (part + 1) * branches] = mixed[
                    j * branches : (j + 1) * branches, part * both : (part + 1) * both
                ]


def contract_first(places, table, cubic):
    count, branches, pairs = cubic.shape
    both = 2 * branches
    return pl.pallas_call(
        first_kernel,
        grid_spec=pltpu.PrefetchScalarGridSpec(
            num_scalar_prefetch=1,
            grid=(count // 2,),
            in_specs=[
                pl.BlockSpec((1, branches, both), lambda t, places: (places[2 * t], 0, 0)),
                pl.BlockSpec((1, branches, both), lambda t, places: (places[2 * t + 1], 0, 0)),
                pl.BlockSpec((2, branches, pairs), lambda t, places: (t, 0, 0)),
            ],
            out_specs=pl.BlockSpec((1, branches, both, both), lambda t, places: (t, 0, 0, 0)),
        ),
        out_shape=jax.ShapeDtypeStruct((count // 2, branches, both, both), BF16),
        compiler_params=pltpu.CompilerParams(vmem_limit_bytes=60 * MIB),
        cost_estimate=pl.CostEstimate(
            flops=2 * count * both * branches * pairs,
            bytes_accessed=2 * count * (both + branches) * pairs,
            transcendentals=0,
        ),
        name="contract_first",
    )(places, table, table, cubic)


def second_kernel(stride, group, second_place, third_place, weights, *refs):
    second_refs, third_refs = refs[: 2 * group], refs[2 * group : 4 * group]
    first_ref, pair_ref, *scratch = refs[4 * group :]
    branches = first_ref.shape[1]
    both = 2 * branches

    def mixer(vec_refs):
        columns = []
        for vec_ref in vec_refs:
            vectors = vec_ref[0].astype(F32).T
            real, imag = vectors[:branches], vectors[branches:]
            columns += [jnp.concatenate([real, imag], 0), jnp.concatenate([-imag, real], 0)]
        return jnp.concatenate(columns, 1).astype(BF16)

    left = lax.broadcasted_iota(jnp.int32, (both, both), 1) < branches
    none = jnp.zeros((both, both), BF16)

    def apart(block):
        return jnp.concatenate([jnp.where(left, block, none), jnp.where(left, none, block)], 0)

    def over_k(pair, third_mixer, j):
        turned = scratch[pair % 2]
        mixed = jnp.dot(
            third_mixer,
            jnp.concatenate([apart(first_ref[pair, j]), apart(first_ref[pair, j + 1])], 1),
            preferred_element_type=F32,
        )
        for half in range(2):
            for part in range(2):
                turned[pl.ds(part * branches + j + half, branches, stride=stride), :] = mixed[
                    part * branches : (part + 1) * branches, half * both : (half + 1) * both
                ]

    def over_j(pair, second_mixer, c, total):
        turned = scratch[pair % 2]
        columns = [
            apart(turned[(c + half) * stride : (c + half) * stride + both, :].astype(BF16))
            for half in range(2)
        ]
        values = jnp.dot(second_mixer, jnp.concatenate(columns, 1), preferred_element_type=F32)
        real, imag = values[:branches], values[branches:]
        power = real * real + imag * imag
        over_b = jnp.sum(power, 0, keepdims=True)
        for half in range(2):
            lanes = slice(half * both, (half + 1) * both)
            total = total + power[:, lanes]
            turned[pl.ds(c + half, 1), :] = over_b[:, lanes]
        return total

    def finish(pair, total):
        first = 2 * (group * pl.program_id(0) + pair)
        near = left[:branches]
        weight = jnp.where(near, weights[first].astype(F32), weights[first + 1].astype(F32))
        for part, parted in enumerate((total, scratch[pair % 2][:branches, :])):
            own = parted * weight
            other = pltpu.roll(own, branches, 1)
            start = part * both
            for t, (upper, lower) in enumerate(((own, other), (other, own))):
                pair_ref[2 * pair + t, start : start + branches, :] = jnp.where(
                    near, upper, 0.0
                ).astype(BF16)
                pair_ref[2 * pair + t, start + branches : start + both, :] = jnp.where(
                    near, 0.0, lower
                ).astype(BF16)

    for phase in range(group + 1):
        before = phase - 1
        if phase < group:
            third_mixer = mixer(third_refs[2 * phase : 2 * phase + 2])
        if phase > 0:
            second_mixer = mixer(second_refs[2 * before : 2 * before + 2])
            total = jnp.zeros((branches, both), F32)
        for at in range(0, branches, 2):
            if phase > 0:
                total = over_j(before, second_mixer, at, total)
            if phase < group:
                over_k(phase, third_mixer, at)
        if phase > 0:
            finish(before, total)


def contract_rest(second_place, third_place, weights, table, first):
    pairs, branches, both = first.shape[:3]
    group = 2 if pairs % 2 == 0 else 1
    stride = both + 9

    def vectors(which, t):
        return pl.BlockSpec(
            (1, branches, both), lambda s, *places: (places[which][2 * group * s + t], 0, 0)
        )

    return pl.pallas_call(
        functools.partial(second_kernel, stride, group),
        grid_spec=pltpu.PrefetchScalarGridSpec(
            num_scalar_prefetch=3,
            grid=(pairs // group,),
            in_specs=[vectors(which, t) for which in range(2) for t in range(2 * group)]
            + [pl.BlockSpec((group, branches, both, both), lambda s, *places: (s, 0, 0, 0))],
            out_specs=pl.BlockSpec((2 * group, 2 * both, both), lambda s, *places: (s, 0, 0)),
            scratch_shapes=[pltpu.VMEM((branches * stride, both), F32)] * 2,
        ),
        out_shape=jax.ShapeDtypeStruct((2 * pairs, 2 * both, both), BF16),
        compiler_params=pltpu.CompilerParams(vmem_limit_bytes=32 * MIB),
        cost_estimate=pl.CostEstimate(
            flops=16 * pairs * both * both * branches * branches,
            bytes_accessed=2 * pairs * both * both * branches,
            transcendentals=0,
        ),
        name="contract_rest",
    )(second_place, third_place, weights, *[table] * (4 * group), first)


def terms_kernel(
    columns, second_place, third_place, row_place, table_ref, pair_ref, *rest
):
    out_refs, packed = rest[:-1], rest[-1]
    rows, lanes = table_ref.shape[1:]
    packed[...] = jnp.zeros_like(packed)
    row = lax.broadcasted_iota(jnp.int32, (rows, lanes), 0)
    lane = lax.broadcasted_iota(jnp.int32, (rows, lanes), 1)
    is_rest = (row == columns - rows + 1) & (lane >= lanes // 2)
    for t in range(pair_ref.shape[0]):
        states = jnp.concatenate([table_ref[second_place[t]], table_ref[third_place[t]]], 1)
        terms = jnp.dot(states, pair_ref[t], preferred_element_type=F32)
        short = terms.astype(BF16).astype(F32)
        terms = jnp.where(is_rest, pltpu.roll(terms - short, 1, 0), terms)
        packed[row_place[t]] = terms.astype(BF16)
    cap = out_refs[0].shape[0]
    for d, out_ref in enumerate(out_refs):
        out_ref[...] = packed[d * cap : (d + 1) * cap]


def coupling_terms(second_place, third_place, row_place, table, pairs, columns, row_count, row_cap):
    rows, lanes = table.shape[1:]
    return pl.pallas_call(
        functools.partial(terms_kernel, columns),
        in_specs=[pl.BlockSpec(memory_space=pltpu.SMEM)] * 3
        + [pl.BlockSpec(memory_space=pltpu.VMEM)] * 2,
        out_specs=[pl.BlockSpec(memory_space=pltpu.VMEM)] * row_count,
        out_shape=[jax.ShapeDtypeStruct((row_cap, rows, lanes), BF16)] * row_count,
        scratch_shapes=[pltpu.VMEM((row_count * row_cap, rows, lanes), BF16)],
        compiler_params=pltpu.CompilerParams(vmem_limit_bytes=16 * MIB),
        name="coupling_terms",
    )(second_place, third_place, row_place, table, pairs)


def update_kernel(columns, first, last, codes, queries, *rest):
    row_count = codes.shape[0]
    arrived, rest = rest[:row_count], rest[row_count:]
    state_ref, source_ref, rate_ref = rest[:3]
    new_ref, next_ref, total = rest[3:]
    homes, rows, lanes = state_ref.shape
    total[...] = jnp.zeros_like(total)
    for d in range(row_count):
        for slot in range(codes.shape[1]):
            code = codes[d, slot]
            total[code] += arrived[d][slot].astype(F32)
    coupled = total[1:]
    if first:
        at = columns - rows
        rate = coupled[:, at : at + 1, :] + coupled[:, at + 1 : at + 2, :]
        lane = lax.broadcasted_iota(jnp.int32, rate.shape, 2)
        rate = jnp.where(lane < lanes // 2, pltpu.roll(rate, lanes // 2, 2), rate)
        rate = jnp.broadcast_to(rate + rate_ref[...], (homes, rows, lanes))
    else:
        rate = rate_ref[...]
    new = (1.0 - DAMPING) * state_ref[...] + DAMPING * (source_ref[...] + coupled) / rate
    new_ref[...] = new
    if first:
        next_ref[0][...] = rate
    if not last:
        send_ref = next_ref[-1]
        for slot in range(queries.shape[0]):
            send_ref[slot] = new_ref[queries[slot]].astype(BF16)


def update(codes, queries, arrived, state, source, rate, columns, first, last):
    homes, rows, lanes = state.shape
    outs = [jax.ShapeDtypeStruct(state.shape, F32)]
    if first:
        outs.append(jax.ShapeDtypeStruct(state.shape, F32))
    if not last:
        outs.append(jax.ShapeDtypeStruct((queries.shape[0], rows, lanes), BF16))
    row_count = len(arrived)

    def kernel(codes, queries, *refs):
        ins = refs[: row_count + 3]
        new_ref = refs[row_count + 3]
        more = refs[row_count + 4 : row_count + 3 + len(outs)]
        update_kernel(columns, first, last, codes, queries, *ins, new_ref, more, refs[-1])

    return pl.pallas_call(
        kernel,
        in_specs=[pl.BlockSpec(memory_space=pltpu.SMEM)] * 2
        + [pl.BlockSpec(memory_space=pltpu.VMEM)] * (row_count + 3),
        out_specs=[pl.BlockSpec(memory_space=pltpu.VMEM)] * len(outs),
        out_shape=outs,
        scratch_shapes=[pltpu.VMEM((homes + 1, rows, lanes), F32)],
        compiler_params=pltpu.CompilerParams(vmem_limit_bytes=16 * MIB),
        name="update",
    )(codes, queries, *arrived, state, source, rate)


def body(eigvecs, cubic, triplets, weights, deviation, source, base_rate):
    row_count = lax.axis_size("row")
    devices = lax.axis_size("trip") * row_count
    home_rows, branches = eigvecs.shape[:2]
    trip_local = cubic.shape[0]
    columns = deviation.shape[1] // branches
    far_cap = (2 * trip_local + devices - 1) // devices
    row_cap = trip_local // 2
    row_slots = row_count * row_cap
    rows = 8 * ((columns + 2 + 15) // 16)

    def packed(values):
        values = jnp.swapaxes(values.reshape(home_rows, branches, columns), 1, 2)
        values = jnp.pad(values, ((0, 0), (0, 2 * rows - columns), (0, 0)))
        values = values.reshape(home_rows, 2, rows, branches)
        return jnp.swapaxes(values, 1, 2).reshape(home_rows, rows, 2 * branches)

    def unpacked(values):
        values = jnp.swapaxes(values.reshape(home_rows, rows, 2, branches), 1, 2)
        values = values.reshape(home_rows, 2 * rows, branches)[:, :columns]
        return jnp.swapaxes(values, 1, 2).reshape(home_rows, branches * columns)

    first_dev = triplets[:, 0] // home_rows
    first_local = triplets[:, 0] - first_dev * home_rows
    ahead = (first_dev - lax.axis_index("row")) % row_count
    row_place = ahead * row_cap + ranks_of(ahead)
    row_codes = pack_ints(row_place, first_local + 1, row_slots).reshape(row_count, row_cap)

    far_index = triplets[:, 1:].reshape(-1)
    far_owner = far_index // home_rows
    far_rank = ranks_of(far_owner)
    far_place = far_owner * far_cap + far_rank
    message = pack_ints(
        far_owner * LANES + far_rank, far_index - far_owner * home_rows, devices * LANES
    ).reshape(devices, 1, LANES)

    def far(values):
        return lax.all_to_all(values, AXES, split_axis=0, concat_axis=0, tiled=True)

    queries = far(message)[:, 0, :far_cap].reshape(-1)
    second_place, third_place = far_place.reshape(trip_local, 2).T
    codes = jnp.stack(from_peers([row_codes[d] for d in range(row_count)]))
    row_vecs = look_up(jnp.maximum(codes - 1, 0).reshape(-1), eigvecs, row_count)
    first_table = jnp.concatenate(
        [row_vecs[0]]
        + [
            lax.ppermute(row_vecs[d], "row", [(i, (i - d) % row_count) for i in range(row_count)])
            for d in range(1, row_count)
        ],
        0,
    )

    state = packed(deviation)
    one = lax.broadcasted_iota(jnp.int32, state.shape[1:], 0) + rows * (
        lax.broadcasted_iota(jnp.int32, state.shape[1:], 1) // branches
    )
    sent_state = jnp.where(one == columns, 1.0, state).astype(BF16)
    records = jnp.concatenate([eigvecs, sent_state], 1)
    queries, first_table = lax.optimization_barrier((queries, first_table))
    far_table = far(look_up(queries, records, 1)[0])
    driven = packed(source)
    rate = jnp.concatenate([base_rate, base_rate], 1)[:, None, :]
    first_table, driven, rate = lax.optimization_barrier((first_table, driven, rate))
    first_part = contract_first(row_place, first_table, cubic)
    arrived_state = far_table[:, branches:]
    pairs = contract_rest(second_place, third_place, weights, far_table, first_part)

    for step in range(ITERS):
        terms = coupling_terms(
            second_place, third_place, row_place, arrived_state, pairs, columns, row_count, row_cap
        )
        arrived = from_peers(terms)
        first, last = step == 0, step == ITERS - 1
        results = update(codes, queries, arrived, state, driven, rate, columns, first, last)
        state = results[0]
        if first:
            rate = results[1]
        if not last:
            arrived_state = far(results[-1])
    return unpacked(state)


def solution(mesh):
    whole = P(AXES, None, None)
    flat = P(AXES, None)
    in_specs = (whole, whole, flat, P(AXES), flat, flat, flat)
    return jax.shard_map(body, mesh=mesh, in_specs=in_specs, out_specs=flat, check_vma=False)
```

```python
import functools

import jax
import jax.numpy as jnp
from jax import lax
from jax.experimental import pallas as pl
from jax.experimental.pallas import tpu as pltpu
from jax.sharding import PartitionSpec as P

ITERS = 2
DAMPING = 0.7
AXES = ("trip", "row")
F32 = jnp.float32
BF16 = jnp.bfloat16
LANES = 128
MIB = 2**20


def ranks_of(target):
    extent = target.shape[0]
    matches = target[:, None] == target[None, :]
    earlier = lax.broadcasted_iota(jnp.int32, (extent, extent), 1) < lax.broadcasted_iota(
        jnp.int32, (extent, extent), 0
    )
    return jnp.sum((matches & earlier).astype(jnp.int32), axis=1)


def pack_ints(places, values, extent):
    onehot = lax.broadcasted_iota(jnp.int32, (extent, places.shape[0]), 0) == places[None, :]
    return jnp.sum(jnp.where(onehot, values[None, :], 0), axis=1)


def from_peers(blocks):
    count = len(blocks)
    return [blocks[0]] + [
        lax.ppermute(blocks[d], "row", [(i, (i + d) % count) for i in range(count)])
        for d in range(1, count)
    ]


def lookup_kernel(queries, table_ref, *found_refs):
    cap = found_refs[0].shape[0]
    for d, found_ref in enumerate(found_refs):
        for slot in range(cap):
            found_ref[slot] = table_ref[queries[d * cap + slot]]


def look_up(queries, table, parts):
    cap = queries.shape[0] // parts
    return pl.pallas_call(
        lookup_kernel,
        in_specs=[
            pl.BlockSpec(memory_space=pltpu.SMEM),
            pl.BlockSpec(memory_space=pltpu.VMEM),
        ],
        out_specs=[pl.BlockSpec(memory_space=pltpu.VMEM)] * parts,
        out_shape=[jax.ShapeDtypeStruct((cap,) + table.shape[1:], table.dtype)] * parts,
        compiler_params=pltpu.CompilerParams(vmem_limit_bytes=16 * MIB),
        name="look_up",
    )(queries, table)


def pick_kernel(which, places, *refs):
    table_refs, out_ref = refs[:-1], refs[-1]
    for t in range(out_ref.shape[0]):
        place, wanted = places[t], which[t]
        found = table_refs[0][place]
        for block in range(1, len(table_refs)):
            found = jnp.where(wanted == block, table_refs[block][place], found)
        out_ref[t] = found


def pick(which, places, tables):
    count = which.shape[0]
    return pl.pallas_call(
        pick_kernel,
        in_specs=[pl.BlockSpec(memory_space=pltpu.SMEM)] * 2
        + [pl.BlockSpec(memory_space=pltpu.VMEM)] * len(tables),
        out_specs=pl.BlockSpec(memory_space=pltpu.VMEM),
        out_shape=jax.ShapeDtypeStruct((count,) + tables[0].shape[1:], tables[0].dtype),
        compiler_params=pltpu.CompilerParams(vmem_limit_bytes=16 * MIB),
        name="pick",
    )(which, places, *tables)


def first_kernel(vec_ref, cubic_ref, out_ref):
    branches = cubic_ref.shape[1]
    both = 2 * branches
    step = 4
    for pair in range(out_ref.shape[0]):
        one, two = vec_ref[2 * pair], vec_ref[2 * pair + 1]
        none = jnp.zeros((branches, branches), one.dtype)
        mixer = jnp.concatenate(
            [
                jnp.concatenate([one[:, :branches], none, one[:, branches:], none], 1),
                jnp.concatenate([none, two[:, :branches], none, two[:, branches:]], 1),
            ],
            0,
        )
        for start in range(0, branches, step):
            lanes = slice(start * branches, (start + step) * branches)
            turned = jnp.concatenate(
                [cubic_ref[2 * pair, :, lanes], cubic_ref[2 * pair + 1, :, lanes]], 0
            ).T
            mixed = jnp.dot(turned, mixer, preferred_element_type=F32).astype(BF16)
            for j in range(step):
                for part in range(2):
                    out_ref[pair, start + j, part * branches : (part + 1) * branches] = mixed[
                        j * branches : (j + 1) * branches, part * both : (part + 1) * both
                    ]


def contract_first(vectors, cubic):
    count, branches, pairs = cubic.shape
    both = 2 * branches
    group = 2 if count % 4 == 0 else 1
    return pl.pallas_call(
        first_kernel,
        grid=(count // (2 * group),),
        in_specs=[
            pl.BlockSpec((2 * group, branches, both), lambda s: (s, 0, 0)),
            pl.BlockSpec((2 * group, branches, pairs), lambda s: (s, 0, 0)),
        ],
        out_specs=pl.BlockSpec((group, branches, both, both), lambda s: (s, 0, 0, 0)),
        out_shape=jax.ShapeDtypeStruct((count // 2, branches, both, both), BF16),
        compiler_params=pltpu.CompilerParams(vmem_limit_bytes=40 * MIB),
        cost_estimate=pl.CostEstimate(
            flops=2 * count * both * branches * pairs,
            bytes_accessed=2 * count * (both + branches) * pairs,
            transcendentals=0,
        ),
        name="contract_first",
    )(vectors, cubic)


def second_kernel(stride, group, second_place, third_place, weights, *refs):
    second_refs, third_refs = refs[: 2 * group], refs[2 * group : 4 * group]
    first_ref, pair_ref, *scratch = refs[4 * group :]
    branches = first_ref.shape[1]
    both = 2 * branches

    def mixer(vec_refs):
        columns = []
        for vec_ref in vec_refs:
            vectors = vec_ref[0].astype(F32).T
            real, imag = vectors[:branches], vectors[branches:]
            columns += [jnp.concatenate([real, imag], 0), jnp.concatenate([-imag, real], 0)]
        return jnp.concatenate(columns, 1).astype(BF16)

    left = lax.broadcasted_iota(jnp.int32, (both, both), 1) < branches
    none = jnp.zeros((both, both), BF16)

    def apart(block):
        return jnp.concatenate([jnp.where(left, block, none), jnp.where(left, none, block)], 0)

    def over_k(pair, third_mixer, j):
        turned = scratch[pair % 2]
        mixed = jnp.dot(
            third_mixer,
            jnp.concatenate([apart(first_ref[pair, j]), apart(first_ref[pair, j + 1])], 1),
            preferred_element_type=F32,
        )
        for half in range(2):
            for part in range(2):
                turned[pl.ds(part * branches + j + half, branches, stride=stride), :] = mixed[
                    part * branches : (part + 1) * branches, half * both : (half + 1) * both
                ]

    def over_j(pair, second_mixer, c, total):
        turned = scratch[pair % 2]
        columns = [
            apart(turned[(c + half) * stride : (c + half) * stride + both, :].astype(BF16))
            for half in range(2)
        ]
        values = jnp.dot(second_mixer, jnp.concatenate(columns, 1), preferred_element_type=F32)
        real, imag = values[:branches], values[branches:]
        power = real * real + imag * imag
        over_b = jnp.sum(power, 0, keepdims=True)
        for half in range(2):
            lanes = slice(half * both, (half + 1) * both)
            total = total + power[:, lanes]
            turned[pl.ds(c + half, 1), :] = over_b[:, lanes]
        return total

    def finish(pair, total):
        first = 2 * (group * pl.program_id(0) + pair)
        near = left[:branches]
        weight = jnp.where(near, weights[first].astype(F32), weights[first + 1].astype(F32))
        for part, parted in enumerate((total, scratch[pair % 2][:branches, :])):
            own = parted * weight
            other = pltpu.roll(own, branches, 1)
            start = part * both
            for t, (upper, lower) in enumerate(((own, other), (other, own))):
                pair_ref[2 * pair + t, start : start + branches, :] = jnp.where(
                    near, upper, 0.0
                ).astype(BF16)
                pair_ref[2 * pair + t, start + branches : start + both, :] = jnp.where(
                    near, 0.0, lower
                ).astype(BF16)

    for phase in range(group + 1):
        before = phase - 1
        if phase < group:
            third_mixer = mixer(third_refs[2 * phase : 2 * phase + 2])
        if phase > 0:
            second_mixer = mixer(second_refs[2 * before : 2 * before + 2])
            total = jnp.zeros((branches, both), F32)
        for at in range(0, branches, 2):
            if phase > 0:
                total = over_j(before, second_mixer, at, total)
            if phase < group:
                over_k(phase, third_mixer, at)
        if phase > 0:
            finish(before, total)


def contract_rest(second_place, third_place, weights, table, first):
    pairs, branches, both = first.shape[:3]
    group = 2 if pairs % 2 == 0 else 1
    stride = both + 9

    def vectors(which, t):
        return pl.BlockSpec(
            (1, branches, both), lambda s, *places: (places[which][2 * group * s + t], 0, 0)
        )

    return pl.pallas_call(
        functools.partial(second_kernel, stride, group),
        grid_spec=pltpu.PrefetchScalarGridSpec(
            num_scalar_prefetch=3,
            grid=(pairs // group,),
            in_specs=[vectors(which, t) for which in range(2) for t in range(2 * group)]
            + [pl.BlockSpec((group, branches, both, both), lambda s, *places: (s, 0, 0, 0))],
            out_specs=pl.BlockSpec((2 * group, 2 * both, both), lambda s, *places: (s, 0, 0)),
            scratch_shapes=[pltpu.VMEM((branches * stride, both), F32)] * 2,
        ),
        out_shape=jax.ShapeDtypeStruct((2 * pairs, 2 * both, both), BF16),
        compiler_params=pltpu.CompilerParams(vmem_limit_bytes=44 * MIB),
        cost_estimate=pl.CostEstimate(
            flops=16 * pairs * both * both * branches * branches,
            bytes_accessed=2 * pairs * both * both * branches,
            transcendentals=0,
        ),
        name="contract_rest",
    )(second_place, third_place, weights, *[table] * (4 * group), first)


def terms_kernel(
    columns, second_place, third_place, row_place, table_ref, pair_ref, *rest
):
    out_refs, packed = rest[:-1], rest[-1]
    rows, lanes = table_ref.shape[1:]
    packed[...] = jnp.zeros_like(packed)
    row = lax.broadcasted_iota(jnp.int32, (rows, lanes), 0)
    lane = lax.broadcasted_iota(jnp.int32, (rows, lanes), 1)
    is_rest = (row == columns - rows + 1) & (lane >= lanes // 2)
    for t in range(pair_ref.shape[0]):
        states = jnp.concatenate([table_ref[second_place[t]], table_ref[third_place[t]]], 1)
        terms = jnp.dot(states, pair_ref[t], preferred_element_type=F32)
        short = terms.astype(BF16).astype(F32)
        terms = jnp.where(is_rest, pltpu.roll(terms - short, 1, 0), terms)
        packed[row_place[t]] = terms.astype(BF16)
    cap = out_refs[0].shape[0]
    for d, out_ref in enumerate(out_refs):
        out_ref[...] = packed[d * cap : (d + 1) * cap]


def coupling_terms(second_place, third_place, row_place, table, pairs, columns, row_count, row_cap):
    rows, lanes = table.shape[1:]
    return pl.pallas_call(
        functools.partial(terms_kernel, columns),
        in_specs=[pl.BlockSpec(memory_space=pltpu.SMEM)] * 3
        + [pl.BlockSpec(memory_space=pltpu.VMEM)] * 2,
        out_specs=[pl.BlockSpec(memory_space=pltpu.VMEM)] * row_count,
        out_shape=[jax.ShapeDtypeStruct((row_cap, rows, lanes), BF16)] * row_count,
        scratch_shapes=[pltpu.VMEM((row_count * row_cap, rows, lanes), BF16)],
        compiler_params=pltpu.CompilerParams(vmem_limit_bytes=16 * MIB),
        name="coupling_terms",
    )(second_place, third_place, row_place, table, pairs)


def update_kernel(columns, first, last, codes, queries, *rest):
    row_count = codes.shape[0]
    arrived, rest = rest[:row_count], rest[row_count:]
    state_ref, source_ref, rate_ref = rest[:3]
    new_ref, next_ref, total = rest[3:]
    homes, rows, lanes = state_ref.shape
    total[...] = jnp.zeros_like(total)
    for d in range(row_count):
        for slot in range(codes.shape[1]):
            code = codes[d, slot]
            total[code] += arrived[d][slot].astype(F32)
    coupled = total[1:]
    if first:
        at = columns - rows
        rate = coupled[:, at : at + 1, :] + coupled[:, at + 1 : at + 2, :]
        lane = lax.broadcasted_iota(jnp.int32, rate.shape, 2)
        rate = jnp.where(lane < lanes // 2, pltpu.roll(rate, lanes // 2, 2), rate)
        rate = jnp.broadcast_to(rate + rate_ref[...], (homes, rows, lanes))
    else:
        rate = rate_ref[...]
    new = (1.0 - DAMPING) * state_ref[...] + DAMPING * (source_ref[...] + coupled) / rate
    new_ref[...] = new
    if first:
        next_ref[0][...] = rate
    if not last:
        send_ref = next_ref[-1]
        for slot in range(queries.shape[0]):
            send_ref[slot] = new_ref[queries[slot]].astype(BF16)


def update(codes, queries, arrived, state, source, rate, columns, first, last):
    homes, rows, lanes = state.shape
    outs = [jax.ShapeDtypeStruct(state.shape, F32)]
    if first:
        outs.append(jax.ShapeDtypeStruct(state.shape, F32))
    if not last:
        outs.append(jax.ShapeDtypeStruct((queries.shape[0], rows, lanes), BF16))
    row_count = len(arrived)

    def kernel(codes, queries, *refs):
        ins = refs[: row_count + 3]
        new_ref = refs[row_count + 3]
        more = refs[row_count + 4 : row_count + 3 + len(outs)]
        update_kernel(columns, first, last, codes, queries, *ins, new_ref, more, refs[-1])

    return pl.pallas_call(
        kernel,
        in_specs=[pl.BlockSpec(memory_space=pltpu.SMEM)] * 2
        + [pl.BlockSpec(memory_space=pltpu.VMEM)] * (row_count + 3),
        out_specs=[pl.BlockSpec(memory_space=pltpu.VMEM)] * len(outs),
        out_shape=outs,
        scratch_shapes=[pltpu.VMEM((homes + 1, rows, lanes), F32)],
        compiler_params=pltpu.CompilerParams(vmem_limit_bytes=16 * MIB),
        name="update",
    )(codes, queries, *arrived, state, source, rate)


def body(eigvecs, cubic, triplets, weights, deviation, source, base_rate):
    row_count = lax.axis_size("row")
    devices = lax.axis_size("trip") * row_count
    home_rows, branches = eigvecs.shape[:2]
    trip_local = cubic.shape[0]
    columns = deviation.shape[1] // branches
    far_cap = (2 * trip_local + devices - 1) // devices
    row_cap = trip_local // 2
    rows = 8 * ((columns + 2 + 15) // 16)

    def packed(values):
        values = jnp.swapaxes(values.reshape(home_rows, branches, columns), 1, 2)
        values = jnp.pad(values, ((0, 0), (0, 2 * rows - columns), (0, 0)))
        values = values.reshape(home_rows, 2, rows, branches)
        return jnp.swapaxes(values, 1, 2).reshape(home_rows, rows, 2 * branches)

    def unpacked(values):
        values = jnp.swapaxes(values.reshape(home_rows, rows, 2, branches), 1, 2)
        values = values.reshape(home_rows, 2 * rows, branches)[:, :columns]
        return jnp.swapaxes(values, 1, 2).reshape(home_rows, branches * columns)

    gathered = {0: eigvecs}
    bit = row_count // 2
    while bit:
        pairing = [(i, i ^ bit) for i in range(row_count)]
        gathered.update({k ^ bit: lax.ppermute(v, "row", pairing) for k, v in gathered.items()})
        bit //= 2

    me = lax.axis_index("trip") * row_count + lax.axis_index("row")
    owner = triplets // home_rows
    local = triplets - owner * home_rows
    first_dev, far_owner = owner[:, 0], owner[:, 1:].reshape(-1)
    row_rank = ranks_of(first_dev)
    far_rank = ranks_of(far_owner)
    message = pack_ints(
        jnp.concatenate([far_owner * LANES + far_rank, first_dev * LANES + far_cap + row_rank]),
        jnp.concatenate([local[:, 1:].reshape(-1), local[:, 0] + 1]),
        devices * LANES,
    ).reshape(devices, 1, LANES)

    def far(values):
        return lax.all_to_all(values, AXES, split_axis=0, concat_axis=0, tiled=True)

    heard = far(message)[:, 0]
    queries = heard[:, :far_cap].reshape(-1)
    row_place = (first_dev - me) % row_count * row_cap + row_rank
    far_place = far_owner * far_cap + far_rank
    second_place, third_place = far_place.reshape(trip_local, 2).T
    asked = lax.dynamic_slice(
        heard, (lax.axis_index("trip") * row_count, far_cap), (row_count, row_cap)
    )
    codes = jnp.take(
        asked, (lax.axis_index("row") - jnp.arange(row_count)) % row_count, axis=0, mode="clip"
    )

    state = packed(deviation)
    one = lax.broadcasted_iota(jnp.int32, state.shape[1:], 0) + rows * (
        lax.broadcasted_iota(jnp.int32, state.shape[1:], 1) // branches
    )
    sent_state = jnp.where(one == columns, 1.0, state).astype(BF16)
    records = jnp.concatenate([eigvecs, sent_state], 1)
    far_table = far(look_up(queries, records, 1)[0])
    first_vecs = pick(
        first_dev % row_count ^ lax.axis_index("row"),
        local[:, 0],
        [gathered[k] for k in range(row_count)],
    )
    driven = packed(source)
    rate = jnp.concatenate([base_rate, base_rate], 1)[:, None, :]
    first_vecs, driven, rate = lax.optimization_barrier((first_vecs, driven, rate))
    first_part = contract_first(first_vecs, cubic)
    arrived_state = far_table[:, branches:]
    pairs = contract_rest(second_place, third_place, weights, far_table, first_part)

    for step in range(ITERS):
        terms = coupling_terms(
            second_place, third_place, row_place, arrived_state, pairs, columns, row_count, row_cap
        )
        arrived = from_peers(terms)
        first, last = step == 0, step == ITERS - 1
        results = update(codes, queries, arrived, state, driven, rate, columns, first, last)
        state = results[0]
        if first:
            rate = results[1]
        if not last:
            arrived_state = far(results[-1])
    return unpacked(state)


def solution(mesh):
    whole = P(AXES, None, None)
    flat = P(AXES, None)
    in_specs = (whole, whole, flat, P(AXES), flat, flat, flat)
    return jax.shard_map(body, mesh=mesh, in_specs=in_specs, out_specs=flat, check_vma=False)
```

```python
import functools

import jax
import jax.numpy as jnp
from jax import lax
from jax.experimental import pallas as pl
from jax.experimental.pallas import tpu as pltpu
from jax.sharding import PartitionSpec as P

ITERS = 2
DAMPING = 0.7
AXES = ("trip", "row")
F32 = jnp.float32
BF16 = jnp.bfloat16
LANES = 128
MIB = 2**20


def ranks_of(target):
    extent = target.shape[0]
    matches = target[:, None] == target[None, :]
    earlier = lax.broadcasted_iota(jnp.int32, (extent, extent), 1) < lax.broadcasted_iota(
        jnp.int32, (extent, extent), 0
    )
    return jnp.sum((matches & earlier).astype(jnp.int32), axis=1)


def pack_ints(places, values, extent):
    onehot = lax.broadcasted_iota(jnp.int32, (extent, places.shape[0]), 0) == places[None, :]
    return jnp.sum(jnp.where(onehot, values[None, :], 0), axis=1)


def from_peers(blocks):
    count = len(blocks)
    return [blocks[0]] + [
        lax.ppermute(blocks[d], "row", [(i, (i + d) % count) for i in range(count)])
        for d in range(1, count)
    ]


def lookup_kernel(far_queries, row_queries, record_ref, vec_ref, far_ref, *row_refs):
    for d, row_ref in enumerate(row_refs):
        for slot in range(row_ref.shape[0]):
            row_ref[slot] = vec_ref[row_queries[d, slot]]
    for slot in range(far_ref.shape[0]):
        far_ref[slot] = record_ref[far_queries[slot]]


def look_up(far_queries, row_queries, records, eigvecs):
    row_count, row_cap = row_queries.shape
    found = pl.pallas_call(
        lookup_kernel,
        in_specs=[pl.BlockSpec(memory_space=pltpu.SMEM)] * 2
        + [pl.BlockSpec(memory_space=pltpu.VMEM)] * 2,
        out_specs=[pl.BlockSpec(memory_space=pltpu.VMEM)] * (1 + row_count),
        out_shape=[
            jax.ShapeDtypeStruct(far_queries.shape + records.shape[1:], records.dtype)
        ]
        + [jax.ShapeDtypeStruct((row_cap,) + eigvecs.shape[1:], eigvecs.dtype)] * row_count,
        compiler_params=pltpu.CompilerParams(vmem_limit_bytes=16 * MIB),
        name="look_up",
    )(far_queries, row_queries, records, eigvecs)
    return found[0], found[1:]


def first_kernel(places, *refs):
    vec_refs, (cubic_ref, out_ref) = refs[:-2], refs[-2:]
    branches = cubic_ref.shape[1]
    both = 2 * branches
    step = 4
    for pair in range(out_ref.shape[0]):
        one, two = vec_refs[2 * pair][0], vec_refs[2 * pair + 1][0]
        none = jnp.zeros((branches, branches), one.dtype)
        mixer = jnp.concatenate(
            [
                jnp.concatenate([one[:, :branches], none, one[:, branches:], none], 1),
                jnp.concatenate([none, two[:, :branches], none, two[:, branches:]], 1),
            ],
            0,
        )
        for start in range(0, branches, step):
            lanes = slice(start * branches, (start + step) * branches)
            turned = jnp.concatenate(
                [cubic_ref[2 * pair, :, lanes], cubic_ref[2 * pair + 1, :, lanes]], 0
            ).T
            mixed = jnp.dot(turned, mixer, preferred_element_type=F32).astype(BF16)
            for j in range(step):
                for part in range(2):
                    out_ref[pair, start + j, part * branches : (part + 1) * branches] = mixed[
                        j * branches : (j + 1) * branches, part * both : (part + 1) * both
                    ]


def contract_first(places, table, cubic):
    count, branches, pairs = cubic.shape
    both = 2 * branches
    group = 2 if count % 4 == 0 else 1

    def vectors(t):
        return pl.BlockSpec((1, branches, both), lambda s, places: (places[2 * group * s + t], 0, 0))

    return pl.pallas_call(
        first_kernel,
        grid_spec=pltpu.PrefetchScalarGridSpec(
            num_scalar_prefetch=1,
            grid=(count // (2 * group),),
            in_specs=[vectors(t) for t in range(2 * group)]
            + [pl.BlockSpec((2 * group, branches, pairs), lambda s, places: (s, 0, 0))],
            out_specs=pl.BlockSpec((group, branches, both, both), lambda s, places: (s, 0, 0, 0)),
        ),
        out_shape=jax.ShapeDtypeStruct((count // 2, branches, both, both), BF16),
        compiler_params=pltpu.CompilerParams(vmem_limit_bytes=40 * MIB),
        cost_estimate=pl.CostEstimate(
            flops=2 * count * both * branches * pairs,
            bytes_accessed=2 * count * (both + branches) * pairs,
            transcendentals=0,
        ),
        name="contract_first",
    )(places, *[table] * (2 * group), cubic)


def second_kernel(stride, group, second_place, third_place, weights, *refs):
    second_refs, third_refs = refs[: 2 * group], refs[2 * group : 4 * group]
    first_ref, pair_ref, *scratch = refs[4 * group :]
    branches = first_ref.shape[1]
    both = 2 * branches

    def mixer(vec_refs):
        columns = []
        for vec_ref in vec_refs:
            vectors = vec_ref[0].astype(F32).T
            real, imag = vectors[:branches], vectors[branches:]
            columns += [jnp.concatenate([real, imag], 0), jnp.concatenate([-imag, real], 0)]
        return jnp.concatenate(columns, 1).astype(BF16)

    left = lax.broadcasted_iota(jnp.int32, (both, both), 1) < branches
    none = jnp.zeros((both, both), BF16)

    def apart(block):
        return jnp.concatenate([jnp.where(left, block, none), jnp.where(left, none, block)], 0)

    def over_k(pair, third_mixer, j):
        turned = scratch[pair % 2]
        mixed = jnp.dot(
            third_mixer,
            jnp.concatenate([apart(first_ref[pair, j]), apart(first_ref[pair, j + 1])], 1),
            preferred_element_type=F32,
        )
        for half in range(2):
            for part in range(2):
                turned[pl.ds(part * branches + j + half, branches, stride=stride), :] = mixed[
                    part * branches : (part + 1) * branches, half * both : (half + 1) * both
                ]

    def over_j(pair, second_mixer, c, total):
        turned = scratch[pair % 2]
        columns = [
            apart(turned[(c + half) * stride : (c + half) * stride + both, :].astype(BF16))
            for half in range(2)
        ]
        values = jnp.dot(second_mixer, jnp.concatenate(columns, 1), preferred_element_type=F32)
        real, imag = values[:branches], values[branches:]
        power = real * real + imag * imag
        over_b = jnp.sum(power, 0, keepdims=True)
        for half in range(2):
            lanes = slice(half * both, (half + 1) * both)
            total = total + power[:, lanes]
            turned[pl.ds(c + half, 1), :] = over_b[:, lanes]
        return total

    def finish(pair, total):
        first = 2 * (group * pl.program_id(0) + pair)
        near = left[:branches]
        weight = jnp.where(near, weights[first].astype(F32), weights[first + 1].astype(F32))
        for part, parted in enumerate((total, scratch[pair % 2][:branches, :])):
            own = parted * weight
            other = pltpu.roll(own, branches, 1)
            start = part * both
            for t, (upper, lower) in enumerate(((own, other), (other, own))):
                pair_ref[2 * pair + t, start : start + branches, :] = jnp.where(
                    near, upper, 0.0
                ).astype(BF16)
                pair_ref[2 * pair + t, start + branches : start + both, :] = jnp.where(
                    near, 0.0, lower
                ).astype(BF16)

    for phase in range(group + 1):
        before = phase - 1
        if phase < group:
            third_mixer = mixer(third_refs[2 * phase : 2 * phase + 2])
        if phase > 0:
            second_mixer = mixer(second_refs[2 * before : 2 * before + 2])
            total = jnp.zeros((branches, both), F32)
        for at in range(0, branches, 2):
            if phase > 0:
                total = over_j(before, second_mixer, at, total)
            if phase < group:
                over_k(phase, third_mixer, at)
        if phase > 0:
            finish(before, total)


def contract_rest(second_place, third_place, weights, table, first):
    pairs, branches, both = first.shape[:3]
    group = 2 if pairs % 2 == 0 else 1
    stride = both + 9

    def vectors(which, t):
        return pl.BlockSpec(
            (1, branches, both), lambda s, *places: (places[which][2 * group * s + t], 0, 0)
        )

    return pl.pallas_call(
        functools.partial(second_kernel, stride, group),
        grid_spec=pltpu.PrefetchScalarGridSpec(
            num_scalar_prefetch=3,
            grid=(pairs // group,),
            in_specs=[vectors(which, t) for which in range(2) for t in range(2 * group)]
            + [pl.BlockSpec((group, branches, both, both), lambda s, *places: (s, 0, 0, 0))],
            out_specs=pl.BlockSpec((2 * group, 2 * both, both), lambda s, *places: (s, 0, 0)),
            scratch_shapes=[pltpu.VMEM((branches * stride, both), F32)] * 2,
        ),
        out_shape=jax.ShapeDtypeStruct((2 * pairs, 2 * both, both), BF16),
        compiler_params=pltpu.CompilerParams(vmem_limit_bytes=44 * MIB),
        cost_estimate=pl.CostEstimate(
            flops=16 * pairs * both * both * branches * branches,
            bytes_accessed=2 * pairs * both * both * branches,
            transcendentals=0,
        ),
        name="contract_rest",
    )(second_place, third_place, weights, *[table] * (4 * group), first)


def terms_kernel(
    columns, second_place, third_place, row_place, table_ref, pair_ref, *rest
):
    out_refs, packed = rest[:-1], rest[-1]
    rows, lanes = table_ref.shape[1:]
    packed[...] = jnp.zeros_like(packed)
    row = lax.broadcasted_iota(jnp.int32, (rows, lanes), 0)
    lane = lax.broadcasted_iota(jnp.int32, (rows, lanes), 1)
    is_rest = (row == columns - rows + 1) & (lane >= lanes // 2)
    for t in range(pair_ref.shape[0]):
        states = jnp.concatenate([table_ref[second_place[t]], table_ref[third_place[t]]], 1)
        terms = jnp.dot(states, pair_ref[t], preferred_element_type=F32)
        short = terms.astype(BF16).astype(F32)
        terms = jnp.where(is_rest, pltpu.roll(terms - short, 1, 0), terms)
        packed[row_place[t]] = terms.astype(BF16)
    cap = out_refs[0].shape[0]
    for d, out_ref in enumerate(out_refs):
        out_ref[...] = packed[d * cap : (d + 1) * cap]


def coupling_terms(second_place, third_place, row_place, table, pairs, columns, row_count, row_cap):
    rows, lanes = table.shape[1:]
    return pl.pallas_call(
        functools.partial(terms_kernel, columns),
        in_specs=[pl.BlockSpec(memory_space=pltpu.SMEM)] * 3
        + [pl.BlockSpec(memory_space=pltpu.VMEM)] * 2,
        out_specs=[pl.BlockSpec(memory_space=pltpu.VMEM)] * row_count,
        out_shape=[jax.ShapeDtypeStruct((row_cap, rows, lanes), BF16)] * row_count,
        scratch_shapes=[pltpu.VMEM((row_count * row_cap, rows, lanes), BF16)],
        compiler_params=pltpu.CompilerParams(vmem_limit_bytes=16 * MIB),
        name="coupling_terms",
    )(second_place, third_place, row_place, table, pairs)


def update_kernel(columns, first, last, codes, queries, *rest):
    row_count = codes.shape[0]
    arrived, rest = rest[:row_count], rest[row_count:]
    state_ref, source_ref, rate_ref = rest[:3]
    new_ref, next_ref, total = rest[3:]
    homes, rows, lanes = state_ref.shape
    total[...] = jnp.zeros_like(total)
    for d in range(row_count):
        for slot in range(codes.shape[1]):
            code = codes[d, slot]
            total[code] += arrived[d][slot].astype(F32)
    coupled = total[1:]
    if first:
        at = columns - rows
        rate = coupled[:, at : at + 1, :] + coupled[:, at + 1 : at + 2, :]
        lane = lax.broadcasted_iota(jnp.int32, rate.shape, 2)
        rate = jnp.where(lane < lanes // 2, pltpu.roll(rate, lanes // 2, 2), rate)
        rate = jnp.broadcast_to(rate + rate_ref[...], (homes, rows, lanes))
    else:
        rate = rate_ref[...]
    new = (1.0 - DAMPING) * state_ref[...] + DAMPING * (source_ref[...] + coupled) / rate
    new_ref[...] = new
    if first:
        next_ref[0][...] = rate
    if not last:
        send_ref = next_ref[-1]
        for slot in range(queries.shape[0]):
            send_ref[slot] = new_ref[queries[slot]].astype(BF16)


def update(codes, queries, arrived, state, source, rate, columns, first, last):
    homes, rows, lanes = state.shape
    outs = [jax.ShapeDtypeStruct(state.shape, F32)]
    if first:
        outs.append(jax.ShapeDtypeStruct(state.shape, F32))
    if not last:
        outs.append(jax.ShapeDtypeStruct((queries.shape[0], rows, lanes), BF16))
    row_count = len(arrived)

    def kernel(codes, queries, *refs):
        ins = refs[: row_count + 3]
        new_ref = refs[row_count + 3]
        more = refs[row_count + 4 : row_count + 3 + len(outs)]
        update_kernel(columns, first, last, codes, queries, *ins, new_ref, more, refs[-1])

    return pl.pallas_call(
        kernel,
        in_specs=[pl.BlockSpec(memory_space=pltpu.SMEM)] * 2
        + [pl.BlockSpec(memory_space=pltpu.VMEM)] * (row_count + 3),
        out_specs=[pl.BlockSpec(memory_space=pltpu.VMEM)] * len(outs),
        out_shape=outs,
        scratch_shapes=[pltpu.VMEM((homes + 1, rows, lanes), F32)],
        compiler_params=pltpu.CompilerParams(vmem_limit_bytes=16 * MIB),
        name="update",
    )(codes, queries, *arrived, state, source, rate)


def body(eigvecs, cubic, triplets, weights, deviation, source, base_rate):
    row_count = lax.axis_size("row")
    devices = lax.axis_size("trip") * row_count
    home_rows, branches = eigvecs.shape[:2]
    trip_local = cubic.shape[0]
    columns = deviation.shape[1] // branches
    far_cap = (2 * trip_local + devices - 1) // devices
    row_cap = trip_local // 2
    rows = 8 * ((columns + 2 + 15) // 16)

    def packed(values):
        values = jnp.swapaxes(values.reshape(home_rows, branches, columns), 1, 2)
        values = jnp.pad(values, ((0, 0), (0, 2 * rows - columns), (0, 0)))
        values = values.reshape(home_rows, 2, rows, branches)
        return jnp.swapaxes(values, 1, 2).reshape(home_rows, rows, 2 * branches)

    def unpacked(values):
        values = jnp.swapaxes(values.reshape(home_rows, rows, 2, branches), 1, 2)
        values = values.reshape(home_rows, 2 * rows, branches)[:, :columns]
        return jnp.swapaxes(values, 1, 2).reshape(home_rows, branches * columns)

    me = lax.axis_index("trip") * row_count + lax.axis_index("row")
    owner = triplets // home_rows
    local = triplets - owner * home_rows
    first_dev, far_owner = owner[:, 0], owner[:, 1:].reshape(-1)
    row_rank = ranks_of(first_dev)
    far_rank = ranks_of(far_owner)
    message = pack_ints(
        jnp.concatenate([far_owner * LANES + far_rank, first_dev * LANES + far_cap + row_rank]),
        jnp.concatenate([local[:, 1:].reshape(-1), local[:, 0] + 1]),
        devices * LANES,
    ).reshape(devices, 1, LANES)

    def far(values):
        return lax.all_to_all(values, AXES, split_axis=0, concat_axis=0, tiled=True)

    heard = far(message)[:, 0]
    queries = heard[:, :far_cap].reshape(-1)
    row_place = (first_dev - me) % row_count * row_cap + row_rank
    far_place = far_owner * far_cap + far_rank
    second_place, third_place = far_place.reshape(trip_local, 2).T
    asked = lax.dynamic_slice(
        heard, (lax.axis_index("trip") * row_count, far_cap), (row_count, row_cap)
    )
    codes = jnp.take(
        asked, (lax.axis_index("row") - jnp.arange(row_count)) % row_count, axis=0, mode="clip"
    )

    state = packed(deviation)
    one = lax.broadcasted_iota(jnp.int32, state.shape[1:], 0) + rows * (
        lax.broadcasted_iota(jnp.int32, state.shape[1:], 1) // branches
    )
    sent_state = jnp.where(one == columns, 1.0, state).astype(BF16)
    records = jnp.concatenate([eigvecs, sent_state], 1)
    far_vecs, row_vecs = look_up(queries, jnp.maximum(codes - 1, 0), records, eigvecs)
    far_table = far(far_vecs)
    first_table = jnp.concatenate(
        [row_vecs[0]]
        + [
            lax.ppermute(row_vecs[d], "row", [(i, (i - d) % row_count) for i in range(row_count)])
            for d in range(1, row_count)
        ],
        0,
    )
    driven = packed(source)
    rate = jnp.concatenate([base_rate, base_rate], 1)[:, None, :]
    first_table, driven, rate = lax.optimization_barrier((first_table, driven, rate))
    first_part = contract_first(row_place, first_table, cubic)
    arrived_state = far_table[:, branches:]
    pairs = contract_rest(second_place, third_place, weights, far_table, first_part)

    for step in range(ITERS):
        terms = coupling_terms(
            second_place, third_place, row_place, arrived_state, pairs, columns, row_count, row_cap
        )
        arrived = from_peers(terms)
        first, last = step == 0, step == ITERS - 1
        results = update(codes, queries, arrived, state, driven, rate, columns, first, last)
        state = results[0]
        if first:
            rate = results[1]
        if not last:
            arrived_state = far(results[-1])
    return unpacked(state)


def solution(mesh):
    whole = P(AXES, None, None)
    flat = P(AXES, None)
    in_specs = (whole, whole, flat, P(AXES), flat, flat, flat)
    return jax.shard_map(body, mesh=mesh, in_specs=in_specs, out_specs=flat, check_vma=False)
```

```python
import functools

import jax
import jax.numpy as jnp
from jax import lax
from jax.experimental import pallas as pl
from jax.experimental.pallas import tpu as pltpu
from jax.sharding import PartitionSpec as P

ITERS = 2
DAMPING = 0.7
AXES = ("trip", "row")
F32 = jnp.float32
BF16 = jnp.bfloat16
LANES = 128
MIB = 2**20


def ranks_of(target):
    extent = target.shape[0]
    matches = target[:, None] == target[None, :]
    earlier = lax.broadcasted_iota(jnp.int32, (extent, extent), 1) < lax.broadcasted_iota(
        jnp.int32, (extent, extent), 0
    )
    return jnp.sum((matches & earlier).astype(jnp.int32), axis=1)


def pack_ints(places, values, extent):
    onehot = lax.broadcasted_iota(jnp.int32, (extent, places.shape[0]), 0) == places[None, :]
    return jnp.sum(jnp.where(onehot, values[None, :], 0), axis=1)


def from_peers(blocks):
    count = len(blocks)
    return [blocks[0]] + [
        lax.ppermute(blocks[d], "row", [(i, (i + d) % count) for i in range(count)])
        for d in range(1, count)
    ]


def lookup_kernel(far_queries, row_queries, record_ref, vec_ref, far_ref, *row_refs):
    for d, row_ref in enumerate(row_refs):
        for slot in range(row_ref.shape[0]):
            row_ref[slot] = vec_ref[row_queries[d, slot]]
    for slot in range(far_ref.shape[0]):
        far_ref[slot] = record_ref[far_queries[slot]]


def look_up(far_queries, row_queries, records, eigvecs):
    row_count, row_cap = row_queries.shape
    found = pl.pallas_call(
        lookup_kernel,
        in_specs=[pl.BlockSpec(memory_space=pltpu.SMEM)] * 2
        + [pl.BlockSpec(memory_space=pltpu.VMEM)] * 2,
        out_specs=[pl.BlockSpec(memory_space=pltpu.VMEM)] * (1 + row_count),
        out_shape=[
            jax.ShapeDtypeStruct(far_queries.shape + records.shape[1:], records.dtype)
        ]
        + [jax.ShapeDtypeStruct((row_cap,) + eigvecs.shape[1:], eigvecs.dtype)] * row_count,
        compiler_params=pltpu.CompilerParams(vmem_limit_bytes=16 * MIB),
        name="look_up",
    )(far_queries, row_queries, records, eigvecs)
    return found[0], found[1:]


def pairs_per_step(pairs):
    return next(group for group in (3, 2, 1) if pairs % group == 0)


def first_kernel(places, *refs):
    vec_refs, (cubic_ref, out_ref) = refs[:-2], refs[-2:]
    group = len(vec_refs) // 2
    branches = cubic_ref.shape[1]
    both = 2 * branches
    step = 4
    for pair in range(group):
        out = group * pl.program_id(0) + pair
        one, two = vec_refs[2 * pair][0], vec_refs[2 * pair + 1][0]
        none = jnp.zeros((branches, branches), one.dtype)
        mixer = jnp.concatenate(
            [
                jnp.concatenate([one[:, :branches], none, one[:, branches:], none], 1),
                jnp.concatenate([none, two[:, :branches], none, two[:, branches:]], 1),
            ],
            0,
        )
        for start in range(0, branches, step):
            lanes = slice(start * branches, (start + step) * branches)
            turned = jnp.concatenate(
                [cubic_ref[2 * pair, :, lanes], cubic_ref[2 * pair + 1, :, lanes]], 0
            ).T
            mixed = jnp.dot(turned, mixer, preferred_element_type=F32).astype(BF16)
            for j in range(step):
                for part in range(2):
                    out_ref[out, start + j, part * branches : (part + 1) * branches] = mixed[
                        j * branches : (j + 1) * branches, part * both : (part + 1) * both
                    ]


def contract_first(places, table, cubic):
    count, branches, pairs = cubic.shape
    both = 2 * branches
    group = pairs_per_step(count // 2)

    def vectors(t):
        return pl.BlockSpec((1, branches, both), lambda s, places: (places[2 * group * s + t], 0, 0))

    return pl.pallas_call(
        first_kernel,
        grid_spec=pltpu.PrefetchScalarGridSpec(
            num_scalar_prefetch=1,
            grid=(count // (2 * group),),
            in_specs=[vectors(t) for t in range(2 * group)]
            + [pl.BlockSpec((2 * group, branches, pairs), lambda s, places: (s, 0, 0))],
            out_specs=pl.BlockSpec(memory_space=pltpu.VMEM),
        ),
        out_shape=pltpu.VMEM((count // 2, branches, both, both), BF16),
        compiler_params=pltpu.CompilerParams(vmem_limit_bytes=30 * MIB),
        cost_estimate=pl.CostEstimate(
            flops=2 * count * both * branches * pairs,
            bytes_accessed=2 * count * (both + branches) * pairs,
            transcendentals=0,
        ),
        name="contract_first",
    )(places, *[table] * (2 * group), cubic)


def second_kernel(stride, group, second_place, third_place, weights, *refs):
    second_refs, third_refs = refs[: 2 * group], refs[2 * group : 4 * group]
    first_ref, pair_ref, *scratch = refs[4 * group :]
    branches = first_ref.shape[1]
    both = 2 * branches

    def mixer(vec_refs):
        columns = []
        for vec_ref in vec_refs:
            vectors = vec_ref[0].astype(F32).T
            real, imag = vectors[:branches], vectors[branches:]
            columns += [jnp.concatenate([real, imag], 0), jnp.concatenate([-imag, real], 0)]
        return jnp.concatenate(columns, 1).astype(BF16)

    left = lax.broadcasted_iota(jnp.int32, (both, both), 1) < branches
    none = jnp.zeros((both, both), BF16)

    def apart(block):
        return jnp.concatenate([jnp.where(left, block, none), jnp.where(left, none, block)], 0)

    def over_k(pair, third_mixer, j):
        turned = scratch[pair % 2]
        at = group * pl.program_id(0) + pair
        mixed = jnp.dot(
            third_mixer,
            jnp.concatenate([apart(first_ref[at, j]), apart(first_ref[at, j + 1])], 1),
            preferred_element_type=F32,
        )
        for half in range(2):
            for part in range(2):
                turned[pl.ds(part * branches + j + half, branches, stride=stride), :] = mixed[
                    part * branches : (part + 1) * branches, half * both : (half + 1) * both
                ]

    def over_j(pair, second_mixer, c, total):
        turned = scratch[pair % 2]
        columns = [
            apart(turned[(c + half) * stride : (c + half) * stride + both, :].astype(BF16))
            for half in range(2)
        ]
        values = jnp.dot(second_mixer, jnp.concatenate(columns, 1), preferred_element_type=F32)
        real, imag = values[:branches], values[branches:]
        power = real * real + imag * imag
        over_b = jnp.sum(power, 0, keepdims=True)
        for half in range(2):
            lanes = slice(half * both, (half + 1) * both)
            total = total + power[:, lanes]
            turned[pl.ds(c + half, 1), :] = over_b[:, lanes]
        return total

    def finish(pair, total):
        first = 2 * (group * pl.program_id(0) + pair)
        near = left[:branches]
        weight = jnp.where(near, weights[first].astype(F32), weights[first + 1].astype(F32))
        for part, parted in enumerate((total, scratch[pair % 2][:branches, :])):
            own = parted * weight
            other = pltpu.roll(own, branches, 1)
            start = part * both
            for t, (upper, lower) in enumerate(((own, other), (other, own))):
                pair_ref[2 * pair + t, start : start + branches, :] = jnp.where(
                    near, upper, 0.0
                ).astype(BF16)
                pair_ref[2 * pair + t, start + branches : start + both, :] = jnp.where(
                    near, 0.0, lower
                ).astype(BF16)

    for phase in range(group + 1):
        before = phase - 1
        if phase < group:
            third_mixer = mixer(third_refs[2 * phase : 2 * phase + 2])
        if phase > 0:
            second_mixer = mixer(second_refs[2 * before : 2 * before + 2])
            total = jnp.zeros((branches, both), F32)
        for at in range(0, branches, 2):
            if phase > 0:
                total = over_j(before, second_mixer, at, total)
            if phase < group:
                over_k(phase, third_mixer, at)
        if phase > 0:
            finish(before, total)


def contract_rest(second_place, third_place, weights, table, first):
    pairs, branches, both = first.shape[:3]
    group = pairs_per_step(pairs)
    stride = both + 9

    def vectors(which, t):
        return pl.BlockSpec(
            (1, branches, both), lambda s, *places: (places[which][2 * group * s + t], 0, 0)
        )

    return pl.pallas_call(
        functools.partial(second_kernel, stride, group),
        grid_spec=pltpu.PrefetchScalarGridSpec(
            num_scalar_prefetch=3,
            grid=(pairs // group,),
            in_specs=[vectors(which, t) for which in range(2) for t in range(2 * group)]
            + [pl.BlockSpec(memory_space=pltpu.VMEM)],
            out_specs=pl.BlockSpec((2 * group, 2 * both, both), lambda s, *places: (s, 0, 0)),
            scratch_shapes=[pltpu.VMEM((branches * stride, both), F32)] * 2,
        ),
        out_shape=jax.ShapeDtypeStruct((2 * pairs, 2 * both, both), BF16),
        compiler_params=pltpu.CompilerParams(vmem_limit_bytes=30 * MIB),
        cost_estimate=pl.CostEstimate(
            flops=16 * pairs * both * both * branches * branches,
            bytes_accessed=2 * pairs * both * both * branches,
            transcendentals=0,
        ),
        name="contract_rest",
    )(second_place, third_place, weights, *[table] * (4 * group), pltpu.with_memory_space_constraint(first, pltpu.VMEM))


def terms_kernel(
    columns, second_place, third_place, row_place, table_ref, pair_ref, *rest
):
    out_refs, packed = rest[:-1], rest[-1]
    rows, lanes = table_ref.shape[1:]
    packed[...] = jnp.zeros_like(packed)
    row = lax.broadcasted_iota(jnp.int32, (rows, lanes), 0)
    lane = lax.broadcasted_iota(jnp.int32, (rows, lanes), 1)
    is_rest = (row == columns - rows + 1) & (lane >= lanes // 2)
    for t in range(pair_ref.shape[0]):
        states = jnp.concatenate([table_ref[second_place[t]], table_ref[third_place[t]]], 1)
        terms = jnp.dot(states, pair_ref[t], preferred_element_type=F32)
        short = terms.astype(BF16).astype(F32)
        terms = jnp.where(is_rest, pltpu.roll(terms - short, 1, 0), terms)
        packed[row_place[t]] = terms.astype(BF16)
    cap = out_refs[0].shape[0]
    for d, out_ref in enumerate(out_refs):
        out_ref[...] = packed[d * cap : (d + 1) * cap]


def coupling_terms(second_place, third_place, row_place, table, pairs, columns, row_count, row_cap):
    rows, lanes = table.shape[1:]
    return pl.pallas_call(
        functools.partial(terms_kernel, columns),
        in_specs=[pl.BlockSpec(memory_space=pltpu.SMEM)] * 3
        + [pl.BlockSpec(memory_space=pltpu.VMEM)] * 2,
        out_specs=[pl.BlockSpec(memory_space=pltpu.VMEM)] * row_count,
        out_shape=[jax.ShapeDtypeStruct((row_cap, rows, lanes), BF16)] * row_count,
        scratch_shapes=[pltpu.VMEM((row_count * row_cap, rows, lanes), BF16)],
        compiler_params=pltpu.CompilerParams(vmem_limit_bytes=16 * MIB),
        name="coupling_terms",
    )(second_place, third_place, row_place, table, pairs)


def update_kernel(columns, first, last, codes, queries, *rest):
    row_count = codes.shape[0]
    arrived, rest = rest[:row_count], rest[row_count:]
    state_ref, source_ref, rate_ref = rest[:3]
    new_ref, next_ref, total = rest[3:]
    homes, rows, lanes = state_ref.shape
    total[...] = jnp.zeros_like(total)
    for d in range(row_count):
        for slot in range(codes.shape[1]):
            code = codes[d, slot]
            total[code] += arrived[d][slot].astype(F32)
    coupled = total[1:]
    if first:
        at = columns - rows
        rate = coupled[:, at : at + 1, :] + coupled[:, at + 1 : at + 2, :]
        lane = lax.broadcasted_iota(jnp.int32, rate.shape, 2)
        rate = jnp.where(lane < lanes // 2, pltpu.roll(rate, lanes // 2, 2), rate)
        rate = jnp.broadcast_to(rate + rate_ref[...], (homes, rows, lanes))
    else:
        rate = rate_ref[...]
    new = (1.0 - DAMPING) * state_ref[...] + DAMPING * (source_ref[...] + coupled) / rate
    new_ref[...] = new
    if first:
        next_ref[0][...] = rate
    if not last:
        send_ref = next_ref[-1]
        for slot in range(queries.shape[0]):
            send_ref[slot] = new_ref[queries[slot]].astype(BF16)


def update(codes, queries, arrived, state, source, rate, columns, first, last):
    homes, rows, lanes = state.shape
    outs = [jax.ShapeDtypeStruct(state.shape, F32)]
    if first:
        outs.append(jax.ShapeDtypeStruct(state.shape, F32))
    if not last:
        outs.append(jax.ShapeDtypeStruct((queries.shape[0], rows, lanes), BF16))
    row_count = len(arrived)

    def kernel(codes, queries, *refs):
        ins = refs[: row_count + 3]
        new_ref = refs[row_count + 3]
        more = refs[row_count + 4 : row_count + 3 + len(outs)]
        update_kernel(columns, first, last, codes, queries, *ins, new_ref, more, refs[-1])

    return pl.pallas_call(
        kernel,
        in_specs=[pl.BlockSpec(memory_space=pltpu.SMEM)] * 2
        + [pl.BlockSpec(memory_space=pltpu.VMEM)] * (row_count + 3),
        out_specs=[pl.BlockSpec(memory_space=pltpu.VMEM)] * len(outs),
        out_shape=outs,
        scratch_shapes=[pltpu.VMEM((homes + 1, rows, lanes), F32)],
        compiler_params=pltpu.CompilerParams(vmem_limit_bytes=16 * MIB),
        name="update",
    )(codes, queries, *arrived, state, source, rate)


def body(eigvecs, cubic, triplets, weights, deviation, source, base_rate):
    row_count = lax.axis_size("row")
    devices = lax.axis_size("trip") * row_count
    home_rows, branches = eigvecs.shape[:2]
    trip_local = cubic.shape[0]
    columns = deviation.shape[1] // branches
    far_cap = (2 * trip_local + devices - 1) // devices
    row_cap = trip_local // 2
    rows = 8 * ((columns + 2 + 15) // 16)

    def packed(values):
        values = jnp.swapaxes(values.reshape(home_rows, branches, columns), 1, 2)
        values = jnp.pad(values, ((0, 0), (0, 2 * rows - columns), (0, 0)))
        values = values.reshape(home_rows, 2, rows, branches)
        return jnp.swapaxes(values, 1, 2).reshape(home_rows, rows, 2 * branches)

    def unpacked(values):
        values = jnp.swapaxes(values.reshape(home_rows, rows, 2, branches), 1, 2)
        values = values.reshape(home_rows, 2 * rows, branches)[:, :columns]
        return jnp.swapaxes(values, 1, 2).reshape(home_rows, branches * columns)

    me = lax.axis_index("trip") * row_count + lax.axis_index("row")
    owner = triplets // home_rows
    local = triplets - owner * home_rows
    first_dev, far_owner = owner[:, 0], owner[:, 1:].reshape(-1)
    row_rank = ranks_of(first_dev)
    far_rank = ranks_of(far_owner)
    message = pack_ints(
        jnp.concatenate([far_owner * LANES + far_rank, first_dev * LANES + far_cap + row_rank]),
        jnp.concatenate([local[:, 1:].reshape(-1), local[:, 0] + 1]),
        devices * LANES,
    ).reshape(devices, 1, LANES)

    def far(values):
        return lax.all_to_all(values, AXES, split_axis=0, concat_axis=0, tiled=True)

    heard = far(message)[:, 0]
    queries = heard[:, :far_cap].reshape(-1)
    row_place = (first_dev - me) % row_count * row_cap + row_rank
    far_place = far_owner * far_cap + far_rank
    second_place, third_place = far_place.reshape(trip_local, 2).T
    asked = lax.dynamic_slice(
        heard, (lax.axis_index("trip") * row_count, far_cap), (row_count, row_cap)
    )
    codes = jnp.take(
        asked, (lax.axis_index("row") - jnp.arange(row_count)) % row_count, axis=0, mode="clip"
    )

    state = packed(deviation)
    one = lax.broadcasted_iota(jnp.int32, state.shape[1:], 0) + rows * (
        lax.broadcasted_iota(jnp.int32, state.shape[1:], 1) // branches
    )
    sent_state = jnp.where(one == columns, 1.0, state).astype(BF16)
    records = jnp.concatenate([eigvecs, sent_state], 1)
    far_vecs, row_vecs = look_up(queries, jnp.maximum(codes - 1, 0), records, eigvecs)
    far_table = far(far_vecs)
    first_vecs = [row_vecs[0]] + [
        lax.ppermute(row_vecs[d], "row", [(i, (i - d) % row_count) for i in range(row_count)])
        for d in range(1, row_count)
    ]
    source, base_rate, first_vecs[1] = lax.optimization_barrier((source, base_rate, first_vecs[1]))
    driven = packed(source)
    rate = jnp.concatenate([base_rate, base_rate], 1)[:, None, :]
    first_table = jnp.concatenate(first_vecs, 0)
    first_table, driven, rate = lax.optimization_barrier((first_table, driven, rate))
    first_part = contract_first(row_place, first_table, cubic)
    arrived_state = far_table[:, branches:]
    pairs = contract_rest(second_place, third_place, weights, far_table, first_part)

    for step in range(ITERS):
        terms = coupling_terms(
            second_place, third_place, row_place, arrived_state, pairs, columns, row_count, row_cap
        )
        arrived = from_peers(terms)
        first, last = step == 0, step == ITERS - 1
        results = update(codes, queries, arrived, state, driven, rate, columns, first, last)
        state = results[0]
        if first:
            rate = results[1]
        if not last:
            arrived_state = far(results[-1])
    return unpacked(state)


def solution(mesh):
    whole = P(AXES, None, None)
    flat = P(AXES, None)
    in_specs = (whole, whole, flat, P(AXES), flat, flat, flat)
    return jax.shard_map(body, mesh=mesh, in_specs=in_specs, out_specs=flat, check_vma=False)
```

```python
import functools

import jax
import jax.numpy as jnp
from jax import lax
from jax.experimental import pallas as pl
from jax.experimental.pallas import tpu as pltpu
from jax.sharding import PartitionSpec as P

ITERS = 2
DAMPING = 0.7
AXES = ("trip", "row")
F32 = jnp.float32
BF16 = jnp.bfloat16
LANES = 128
MIB = 2**20


def ranks_of(target):
    extent = target.shape[0]
    matches = target[:, None] == target[None, :]
    earlier = lax.broadcasted_iota(jnp.int32, (extent, extent), 1) < lax.broadcasted_iota(
        jnp.int32, (extent, extent), 0
    )
    return jnp.sum((matches & earlier).astype(jnp.int32), axis=1)


def pack_ints(places, values, extent):
    onehot = lax.broadcasted_iota(jnp.int32, (extent, places.shape[0]), 0) == places[None, :]
    return jnp.sum(jnp.where(onehot, values[None, :], 0), axis=1)


def from_peers(blocks):
    count = len(blocks)
    return [blocks[0]] + [
        lax.ppermute(blocks[d], "row", [(i, (i + d) % count) for i in range(count)])
        for d in range(1, count)
    ]


def lookup_kernel(far_queries, row_queries, record_ref, vec_ref, far_ref, *row_refs):
    for d, row_ref in enumerate(row_refs):
        for slot in range(row_ref.shape[0]):
            row_ref[slot] = vec_ref[row_queries[d, slot]]
    for slot in range(far_ref.shape[0]):
        far_ref[slot] = record_ref[far_queries[slot]]


def look_up(far_queries, row_queries, records, eigvecs):
    row_count, row_cap = row_queries.shape
    found = pl.pallas_call(
        lookup_kernel,
        in_specs=[pl.BlockSpec(memory_space=pltpu.SMEM)] * 2
        + [pl.BlockSpec(memory_space=pltpu.VMEM)] * 2,
        out_specs=[pl.BlockSpec(memory_space=pltpu.VMEM)] * (1 + row_count),
        out_shape=[
            jax.ShapeDtypeStruct(far_queries.shape + records.shape[1:], records.dtype)
        ]
        + [jax.ShapeDtypeStruct((row_cap,) + eigvecs.shape[1:], eigvecs.dtype)] * row_count,
        compiler_params=pltpu.CompilerParams(vmem_limit_bytes=16 * MIB),
        name="look_up",
    )(far_queries, row_queries, records, eigvecs)
    return found[0], found[1:]


def pairs_per_step(pairs):
    return next(group for group in (3, 2, 1) if pairs % group == 0)


def first_kernel(places, *refs):
    vec_refs, (cubic_ref, out_ref) = refs[:-2], refs[-2:]
    group = len(vec_refs) // 2
    branches = cubic_ref.shape[1]
    both = 2 * branches
    step = 4
    for pair in range(group):
        one, two = vec_refs[2 * pair][0], vec_refs[2 * pair + 1][0]
        none = jnp.zeros((branches, branches), one.dtype)
        mixer = jnp.concatenate(
            [
                jnp.concatenate([one[:, :branches], none, one[:, branches:], none], 1),
                jnp.concatenate([none, two[:, :branches], none, two[:, branches:]], 1),
            ],
            0,
        )
        for start in range(0, branches, step):
            lanes = slice(start * branches, (start + step) * branches)
            turned = jnp.concatenate(
                [cubic_ref[2 * pair, :, lanes], cubic_ref[2 * pair + 1, :, lanes]], 0
            ).T
            mixed = jnp.dot(turned, mixer, preferred_element_type=F32).astype(BF16)
            for j in range(step):
                for part in range(2):
                    out_ref[pair, start + j, part * branches : (part + 1) * branches] = mixed[
                        j * branches : (j + 1) * branches, part * both : (part + 1) * both
                    ]


def contract_first(places, table, cubic):
    count, branches, pairs = cubic.shape
    both = 2 * branches
    group = pairs_per_step(count // 2)

    def vectors(t):
        return pl.BlockSpec((1, branches, both), lambda s, places: (places[2 * group * s + t], 0, 0))

    return pl.pallas_call(
        first_kernel,
        grid_spec=pltpu.PrefetchScalarGridSpec(
            num_scalar_prefetch=1,
            grid=(count // (2 * group),),
            in_specs=[vectors(t) for t in range(2 * group)]
            + [pl.BlockSpec((2 * group, branches, pairs), lambda s, places: (s, 0, 0))],
            out_specs=pl.BlockSpec((group, branches, both, both), lambda s, places: (s, 0, 0, 0)),
        ),
        out_shape=jax.ShapeDtypeStruct((count // 2, branches, both, both), BF16),
        compiler_params=pltpu.CompilerParams(vmem_limit_bytes=60 * MIB),
        cost_estimate=pl.CostEstimate(
            flops=20 * 2 * count * both * branches * pairs,
            bytes_accessed=2 * count * (both + branches) * pairs,
            transcendentals=0,
        ),
        name="contract_first",
    )(places, *[table] * (2 * group), cubic)


def second_kernel(stride, group, second_place, third_place, weights, *refs):
    second_refs, third_refs = refs[: 2 * group], refs[2 * group : 4 * group]
    first_ref, pair_ref, *scratch = refs[4 * group :]
    branches = first_ref.shape[1]
    both = 2 * branches

    def mixer(vec_refs):
        columns = []
        for vec_ref in vec_refs:
            vectors = vec_ref[0].astype(F32).T
            real, imag = vectors[:branches], vectors[branches:]
            columns += [jnp.concatenate([real, imag], 0), jnp.concatenate([-imag, real], 0)]
        return jnp.concatenate(columns, 1).astype(BF16)

    left = lax.broadcasted_iota(jnp.int32, (both, both), 1) < branches
    none = jnp.zeros((both, both), BF16)

    def apart(block):
        return jnp.concatenate([jnp.where(left, block, none), jnp.where(left, none, block)], 0)

    def over_k(pair, third_mixer, j):
        turned = scratch[pair % 2]
        mixed = jnp.dot(
            third_mixer,
            jnp.concatenate([apart(first_ref[pair, j]), apart(first_ref[pair, j + 1])], 1),
            preferred_element_type=F32,
        )
        for half in range(2):
            for part in range(2):
                turned[pl.ds(part * branches + j + half, branches, stride=stride), :] = mixed[
                    part * branches : (part + 1) * branches, half * both : (half + 1) * both
                ]

    def over_j(pair, second_mixer, c, total):
        turned = scratch[pair % 2]
        columns = [
            apart(turned[(c + half) * stride : (c + half) * stride + both, :].astype(BF16))
            for half in range(2)
        ]
        values = jnp.dot(second_mixer, jnp.concatenate(columns, 1), preferred_element_type=F32)
        real, imag = values[:branches], values[branches:]
        power = real * real + imag * imag
        over_b = jnp.sum(power, 0, keepdims=True)
        for half in range(2):
            lanes = slice(half * both, (half + 1) * both)
            total = total + power[:, lanes]
            turned[pl.ds(c + half, 1), :] = over_b[:, lanes]
        return total

    def finish(pair, total):
        first = 2 * (group * pl.program_id(0) + pair)
        near = left[:branches]
        weight = jnp.where(near, weights[first].astype(F32), weights[first + 1].astype(F32))
        for part, parted in enumerate((total, scratch[pair % 2][:branches, :])):
            own = parted * weight
            other = pltpu.roll(own, branches, 1)
            start = part * both
            for t, (upper, lower) in enumerate(((own, other), (other, own))):
                pair_ref[2 * pair + t, start : start + branches, :] = jnp.where(
                    near, upper, 0.0
                ).astype(BF16)
                pair_ref[2 * pair + t, start + branches : start + both, :] = jnp.where(
                    near, 0.0, lower
                ).astype(BF16)

    for phase in range(group + 1):
        before = phase - 1
        if phase < group:
            third_mixer = mixer(third_refs[2 * phase : 2 * phase + 2])
        if phase > 0:
            second_mixer = mixer(second_refs[2 * before : 2 * before + 2])
            total = jnp.zeros((branches, both), F32)
        for at in range(0, branches, 2):
            if phase > 0:
                total = over_j(before, second_mixer, at, total)
            if phase < group:
                over_k(phase, third_mixer, at)
        if phase > 0:
            finish(before, total)


def contract_rest(second_place, third_place, weights, table, first):
    pairs, branches, both = first.shape[:3]
    group = pairs_per_step(pairs)
    stride = both + 9

    def vectors(which, t):
        return pl.BlockSpec(
            (1, branches, both), lambda s, *places: (places[which][2 * group * s + t], 0, 0)
        )

    return pl.pallas_call(
        functools.partial(second_kernel, stride, group),
        grid_spec=pltpu.PrefetchScalarGridSpec(
            num_scalar_prefetch=3,
            grid=(pairs // group,),
            in_specs=[vectors(which, t) for which in range(2) for t in range(2 * group)]
            + [pl.BlockSpec((group, branches, both, both), lambda s, *places: (s, 0, 0, 0))],
            out_specs=pl.BlockSpec((2 * group, 2 * both, both), lambda s, *places: (s, 0, 0)),
            scratch_shapes=[pltpu.VMEM((branches * stride, both), F32)] * 2,
        ),
        out_shape=jax.ShapeDtypeStruct((2 * pairs, 2 * both, both), BF16),
        compiler_params=pltpu.CompilerParams(vmem_limit_bytes=44 * MIB),
        cost_estimate=pl.CostEstimate(
            flops=16 * pairs * both * both * branches * branches,
            bytes_accessed=2 * pairs * both * both * branches,
            transcendentals=0,
        ),
        name="contract_rest",
    )(second_place, third_place, weights, *[table] * (4 * group), first)


def terms_kernel(
    columns, second_place, third_place, row_place, table_ref, pair_ref, *rest
):
    out_refs, packed = rest[:-1], rest[-1]
    rows, lanes = table_ref.shape[1:]
    packed[...] = jnp.zeros_like(packed)
    row = lax.broadcasted_iota(jnp.int32, (rows, lanes), 0)
    lane = lax.broadcasted_iota(jnp.int32, (rows, lanes), 1)
    is_rest = (row == columns - rows + 1) & (lane >= lanes // 2)
    for t in range(pair_ref.shape[0]):
        states = jnp.concatenate([table_ref[second_place[t]], table_ref[third_place[t]]], 1)
        terms = jnp.dot(states, pair_ref[t], preferred_element_type=F32)
        short = terms.astype(BF16).astype(F32)
        terms = jnp.where(is_rest, pltpu.roll(terms - short, 1, 0), terms)
        packed[row_place[t]] = terms.astype(BF16)
    cap = out_refs[0].shape[0]
    for d, out_ref in enumerate(out_refs):
        out_ref[...] = packed[d * cap : (d + 1) * cap]


def coupling_terms(second_place, third_place, row_place, table, pairs, columns, row_count, row_cap):
    rows, lanes = table.shape[1:]
    return pl.pallas_call(
        functools.partial(terms_kernel, columns),
        in_specs=[pl.BlockSpec(memory_space=pltpu.SMEM)] * 3
        + [pl.BlockSpec(memory_space=pltpu.VMEM)] * 2,
        out_specs=[pl.BlockSpec(memory_space=pltpu.VMEM)] * row_count,
        out_shape=[jax.ShapeDtypeStruct((row_cap, rows, lanes), BF16)] * row_count,
        scratch_shapes=[pltpu.VMEM((row_count * row_cap, rows, lanes), BF16)],
        compiler_params=pltpu.CompilerParams(vmem_limit_bytes=16 * MIB),
        name="coupling_terms",
    )(second_place, third_place, row_place, table, pairs)


def update_kernel(columns, first, last, codes, queries, *rest):
    row_count = codes.shape[0]
    arrived, rest = rest[:row_count], rest[row_count:]
    state_ref, source_ref, rate_ref = rest[:3]
    new_ref, next_ref, total = rest[3:]
    homes, rows, lanes = state_ref.shape
    total[...] = jnp.zeros_like(total)
    for d in range(row_count):
        for slot in range(codes.shape[1]):
            code = codes[d, slot]
            total[code] += arrived[d][slot].astype(F32)
    coupled = total[1:]
    if first:
        at = columns - rows
        rate = coupled[:, at : at + 1, :] + coupled[:, at + 1 : at + 2, :]
        lane = lax.broadcasted_iota(jnp.int32, rate.shape, 2)
        rate = jnp.where(lane < lanes // 2, pltpu.roll(rate, lanes // 2, 2), rate)
        rate = jnp.broadcast_to(rate + rate_ref[...], (homes, rows, lanes))
    else:
        rate = rate_ref[...]
    new = (1.0 - DAMPING) * state_ref[...] + DAMPING * (source_ref[...] + coupled) / rate
    new_ref[...] = new
    if first:
        next_ref[0][...] = rate
    if not last:
        send_ref = next_ref[-1]
        for slot in range(queries.shape[0]):
            send_ref[slot] = new_ref[queries[slot]].astype(BF16)


def update(codes, queries, arrived, state, source, rate, columns, first, last):
    homes, rows, lanes = state.shape
    outs = [jax.ShapeDtypeStruct(state.shape, F32)]
    if first:
        outs.append(jax.ShapeDtypeStruct(state.shape, F32))
    if not last:
        outs.append(jax.ShapeDtypeStruct((queries.shape[0], rows, lanes), BF16))
    row_count = len(arrived)

    def kernel(codes, queries, *refs):
        ins = refs[: row_count + 3]
        new_ref = refs[row_count + 3]
        more = refs[row_count + 4 : row_count + 3 + len(outs)]
        update_kernel(columns, first, last, codes, queries, *ins, new_ref, more, refs[-1])

    return pl.pallas_call(
        kernel,
        in_specs=[pl.BlockSpec(memory_space=pltpu.SMEM)] * 2
        + [pl.BlockSpec(memory_space=pltpu.VMEM)] * (row_count + 3),
        out_specs=[pl.BlockSpec(memory_space=pltpu.VMEM)] * len(outs),
        out_shape=outs,
        scratch_shapes=[pltpu.VMEM((homes + 1, rows, lanes), F32)],
        compiler_params=pltpu.CompilerParams(vmem_limit_bytes=16 * MIB),
        name="update",
    )(codes, queries, *arrived, state, source, rate)


def body(eigvecs, cubic, triplets, weights, deviation, source, base_rate):
    row_count = lax.axis_size("row")
    devices = lax.axis_size("trip") * row_count
    home_rows, branches = eigvecs.shape[:2]
    trip_local = cubic.shape[0]
    columns = deviation.shape[1] // branches
    far_cap = (2 * trip_local + devices - 1) // devices
    row_cap = trip_local // 2
    rows = 8 * ((columns + 2 + 15) // 16)

    def packed(values):
        values = jnp.swapaxes(values.reshape(home_rows, branches, columns), 1, 2)
        values = jnp.pad(values, ((0, 0), (0, 2 * rows - columns), (0, 0)))
        values = values.reshape(home_rows, 2, rows, branches)
        return jnp.swapaxes(values, 1, 2).reshape(home_rows, rows, 2 * branches)

    def unpacked(values):
        values = jnp.swapaxes(values.reshape(home_rows, rows, 2, branches), 1, 2)
        values = values.reshape(home_rows, 2 * rows, branches)[:, :columns]
        return jnp.swapaxes(values, 1, 2).reshape(home_rows, branches * columns)

    me = lax.axis_index("trip") * row_count + lax.axis_index("row")
    owner = triplets // home_rows
    local = triplets - owner * home_rows
    first_dev, far_owner = owner[:, 0], owner[:, 1:].reshape(-1)
    row_rank = ranks_of(first_dev)
    far_rank = ranks_of(far_owner)
    message = pack_ints(
        jnp.concatenate([far_owner * LANES + far_rank, first_dev * LANES + far_cap + row_rank]),
        jnp.concatenate([local[:, 1:].reshape(-1), local[:, 0] + 1]),
        devices * LANES,
    ).reshape(devices, 1, LANES)

    def far(values):
        return lax.all_to_all(values, AXES, split_axis=0, concat_axis=0, tiled=True)

    heard = far(message)[:, 0]
    queries = heard[:, :far_cap].reshape(-1)
    row_place = (first_dev - me) % row_count * row_cap + row_rank
    far_place = far_owner * far_cap + far_rank
    second_place, third_place = far_place.reshape(trip_local, 2).T
    asked = lax.dynamic_slice(
        heard, (lax.axis_index("trip") * row_count, far_cap), (row_count, row_cap)
    )
    codes = jnp.take(
        asked, (lax.axis_index("row") - jnp.arange(row_count)) % row_count, axis=0, mode="clip"
    )

    state = packed(deviation)
    one = lax.broadcasted_iota(jnp.int32, state.shape[1:], 0) + rows * (
        lax.broadcasted_iota(jnp.int32, state.shape[1:], 1) // branches
    )
    sent_state = jnp.where(one == columns, 1.0, state).astype(BF16)
    records = jnp.concatenate([eigvecs, sent_state], 1)
    far_vecs, row_vecs = look_up(queries, jnp.maximum(codes - 1, 0), records, eigvecs)
    far_table = far(far_vecs)
    first_vecs = [row_vecs[0]] + [
        lax.ppermute(row_vecs[d], "row", [(i, (i - d) % row_count) for i in range(row_count)])
        for d in range(1, row_count)
    ]
    source, base_rate, first_vecs[1] = lax.optimization_barrier((source, base_rate, first_vecs[1]))
    driven = packed(source)
    rate = jnp.concatenate([base_rate, base_rate], 1)[:, None, :]
    first_table = jnp.concatenate(first_vecs, 0)
    first_table, driven, rate = lax.optimization_barrier((first_table, driven, rate))
    first_part = contract_first(row_place, first_table, cubic)
    arrived_state = far_table[:, branches:]
    pairs = contract_rest(second_place, third_place, weights, far_table, first_part)

    for step in range(ITERS):
        terms = coupling_terms(
            second_place, third_place, row_place, arrived_state, pairs, columns, row_count, row_cap
        )
        arrived = from_peers(terms)
        first, last = step == 0, step == ITERS - 1
        results = update(codes, queries, arrived, state, driven, rate, columns, first, last)
        state = results[0]
        if first:
            rate = results[1]
        if not last:
            arrived_state = far(results[-1])
    return unpacked(state)


def solution(mesh):
    whole = P(AXES, None, None)
    flat = P(AXES, None)
    in_specs = (whole, whole, flat, P(AXES), flat, flat, flat)
    return jax.shard_map(body, mesh=mesh, in_specs=in_specs, out_specs=flat, check_vma=False)
```

```python
import functools

import jax
import jax.numpy as jnp
from jax import lax
from jax.experimental import pallas as pl
from jax.experimental.pallas import tpu as pltpu
from jax.sharding import PartitionSpec as P

ITERS = 2
DAMPING = 0.7
AXES = ("trip", "row")
F32 = jnp.float32
BF16 = jnp.bfloat16
LANES = 128
MIB = 2**20


def prepare_kernel(home_rows, far_cap, row_count, row_cap, triplets_ref, message_ref, places_ref):
    count, devices = triplets_ref.shape[1], message_ref.shape[0]
    sub = lax.broadcasted_iota(jnp.int32, (count, count), 0)
    lane = lax.broadcasted_iota(jnp.int32, (count, count), 1)
    same, earlier = sub == lane, sub < lane

    def whole_part(values, size):
        return jnp.floor((values.astype(F32) + 0.5) * (1.0 / size)).astype(jnp.int32)

    wanted = [triplets_ref[which : which + 1, :] for which in range(3)]
    owner = [whole_part(values, home_rows) for values in wanted]
    local = [values - own * home_rows for values, own in zip(wanted, owner)]
    upright = [jnp.sum(jnp.where(same, own, 0), 1, keepdims=True) for own in owner]

    def matches(one, two, mask):
        return (mask & (upright[one] == owner[two])).astype(jnp.int32)

    rank = [
        jnp.sum(found, 0, keepdims=True)
        for found in (
            matches(0, 0, earlier),
            matches(1, 1, earlier) + matches(2, 1, earlier),
            matches(1, 2, earlier | same) + matches(2, 2, earlier),
        )
    ]
    device = lax.broadcasted_iota(jnp.int32, (devices, count), 0)
    slot = lax.broadcasted_iota(jnp.int32, (LANES, count), 0)
    kind, precision = (
        (BF16, None) if home_rows <= 256 else (F32, lax.Precision.HIGHEST)
    )
    message = jnp.zeros((devices, LANES), F32)
    for which in range(3):
        value, at = (local[0] + 1, rank[0] + far_cap) if which == 0 else (local[which], rank[which])
        message = message + lax.dot_general(
            jnp.where(device == owner[which], 1.0, 0.0).astype(kind),
            jnp.where(slot == at, value.astype(F32), 0.0).astype(kind),
            (((1,), (1,)), ((), ())),
            precision=precision,
            preferred_element_type=F32,
        )
    message_ref[...] = (message + 0.5).astype(jnp.int32)
    apart = (owner[0] - row_count * whole_part(owner[0], row_count)) ^ lax.axis_index("row")
    places_ref[...] = jnp.zeros_like(places_ref)
    places_ref[0:1, :count] = apart * row_cap + rank[0]
    for which in range(1, 3):
        places_ref[which : which + 1, :count] = owner[which] * far_cap + rank[which]


def prepare(triplets, home_rows, devices, far_cap, row_count, row_cap):
    return pl.pallas_call(
        functools.partial(prepare_kernel, home_rows, far_cap, row_count, row_cap),
        in_specs=[pl.BlockSpec(memory_space=pltpu.VMEM)],
        out_specs=[pl.BlockSpec(memory_space=pltpu.VMEM)] * 2,
        out_shape=[
            jax.ShapeDtypeStruct((devices, LANES), jnp.int32),
            jax.ShapeDtypeStruct((8, LANES), jnp.int32),
        ],
        name="prepare",
    )(triplets.T)


def to_peer(values, bits, count):
    return lax.ppermute(values, "row", [(i, i ^ bits) for i in range(count)])


def from_peers(blocks):
    return [blocks[0]] + [to_peer(blocks[k], k, len(blocks)) for k in range(1, len(blocks))]


def lookup_kernel(far_cap, row_count, heard, record_ref, vec_ref, far_ref, near_ref, away_ref):
    half = row_count // 2
    cap = near_ref.shape[0] // half
    base = lax.axis_index("trip") * row_count
    for k in range(row_count):
        peer = base + (lax.axis_index("row") ^ k)
        row_ref = near_ref if k < half else away_ref
        for slot in range(cap):
            code = heard[peer, far_cap + slot]
            row_ref[k % half * cap + slot] = vec_ref[jnp.maximum(code - 1, 0)]
    for slot in range(far_ref.shape[0]):
        far_ref[slot] = record_ref[heard[slot // far_cap, slot % far_cap]]


def look_up(heard, records, eigvecs, far_cap, row_count, row_cap):
    row_shape = (row_count // 2 * row_cap,) + eigvecs.shape[1:]
    return pl.pallas_call(
        functools.partial(lookup_kernel, far_cap, row_count),
        in_specs=[pl.BlockSpec(memory_space=pltpu.SMEM)]
        + [pl.BlockSpec(memory_space=pltpu.VMEM)] * 2,
        out_specs=[pl.BlockSpec(memory_space=pltpu.VMEM)] * 3,
        out_shape=[
            jax.ShapeDtypeStruct((heard.shape[0] * far_cap,) + records.shape[1:], records.dtype)
        ]
        + [jax.ShapeDtypeStruct(row_shape, eigvecs.dtype)] * 2,
        compiler_params=pltpu.CompilerParams(vmem_limit_bytes=16 * MIB),
        name="look_up",
    )(heard, records, eigvecs)


def pairs_per_step(pairs):
    return next(group for group in (3, 2, 1) if pairs % group == 0)


def first_kernel(places, *refs):
    vec_refs, (cubic_ref, out_ref) = refs[:-2], refs[-2:]
    group = len(vec_refs) // 2
    branches = cubic_ref.shape[1]
    both = 2 * branches
    step = 4
    for pair in range(group):
        one, two = vec_refs[2 * pair][0], vec_refs[2 * pair + 1][0]
        none = jnp.zeros((branches, branches), one.dtype)
        mixer = jnp.concatenate(
            [
                jnp.concatenate([one[:, :branches], none, one[:, branches:], none], 1),
                jnp.concatenate([none, two[:, :branches], none, two[:, branches:]], 1),
            ],
            0,
        )
        for start in range(0, branches, step):
            lanes = slice(start * branches, (start + step) * branches)
            turned = jnp.concatenate(
                [cubic_ref[2 * pair, :, lanes], cubic_ref[2 * pair + 1, :, lanes]], 0
            ).T
            mixed = jnp.dot(turned, mixer, preferred_element_type=F32).astype(BF16)
            for j in range(step):
                for part in range(2):
                    out_ref[pair, start + j, part * branches : (part + 1) * branches] = mixed[
                        j * branches : (j + 1) * branches, part * both : (part + 1) * both
                    ]


def contract_first(places, table, cubic):
    count, branches, pairs = cubic.shape
    both = 2 * branches
    group = pairs_per_step(count // 2)

    def vectors(t):
        return pl.BlockSpec((1, branches, both), lambda s, places: (places[0, 2 * group * s + t], 0, 0))

    return pl.pallas_call(
        first_kernel,
        grid_spec=pltpu.PrefetchScalarGridSpec(
            num_scalar_prefetch=1,
            grid=(count // (2 * group),),
            in_specs=[vectors(t) for t in range(2 * group)]
            + [pl.BlockSpec((2 * group, branches, pairs), lambda s, places: (s, 0, 0))],
            out_specs=pl.BlockSpec((group, branches, both, both), lambda s, places: (s, 0, 0, 0)),
        ),
        out_shape=jax.ShapeDtypeStruct((count // 2, branches, both, both), BF16),
        compiler_params=pltpu.CompilerParams(vmem_limit_bytes=40 * MIB),
        cost_estimate=pl.CostEstimate(
            flops=8 * 2 * count * both * branches * pairs,
            bytes_accessed=2 * count * (both + branches) * pairs,
            transcendentals=0,
        ),
        name="contract_first",
    )(places, *[table] * (2 * group), cubic)


def second_kernel(stride, group, places, weights, *refs):
    table_ref, first_ref, pair_ref, *scratch = refs
    branches = first_ref.shape[1]
    both = 2 * branches

    def mixer(which, pair):
        columns = []
        for t in range(2):
            place = places[which, 2 * (group * pl.program_id(0) + pair) + t]
            vectors = table_ref[place, :branches].astype(F32).T
            real, imag = vectors[:branches], vectors[branches:]
            columns += [jnp.concatenate([real, imag], 0), jnp.concatenate([-imag, real], 0)]
        return jnp.concatenate(columns, 1).astype(BF16)

    left = lax.broadcasted_iota(jnp.int32, (both, both), 1) < branches
    none = jnp.zeros((both, both), BF16)

    def apart(block):
        return jnp.concatenate([jnp.where(left, block, none), jnp.where(left, none, block)], 0)

    def over_k(pair, third_mixer, j):
        turned = scratch[pair % 2]
        mixed = jnp.dot(
            third_mixer,
            jnp.concatenate([apart(first_ref[pair, j]), apart(first_ref[pair, j + 1])], 1),
            preferred_element_type=F32,
        )
        for half in range(2):
            for part in range(2):
                turned[pl.ds(part * branches + j + half, branches, stride=stride), :] = mixed[
                    part * branches : (part + 1) * branches, half * both : (half + 1) * both
                ]

    def over_j(pair, second_mixer, c, total):
        turned = scratch[pair % 2]
        columns = [
            apart(turned[(c + half) * stride : (c + half) * stride + both, :].astype(BF16))
            for half in range(2)
        ]
        values = jnp.dot(second_mixer, jnp.concatenate(columns, 1), preferred_element_type=F32)
        real, imag = values[:branches], values[branches:]
        power = real * real + imag * imag
        over_b = jnp.sum(power, 0, keepdims=True)
        for half in range(2):
            lanes = slice(half * both, (half + 1) * both)
            total = total + power[:, lanes]
            turned[pl.ds(c + half, 1), :] = over_b[:, lanes]
        return total

    def finish(pair, total):
        first = 2 * (group * pl.program_id(0) + pair)
        near = left[:branches]
        weight = jnp.where(near, weights[first].astype(F32), weights[first + 1].astype(F32))
        for part, parted in enumerate((total, scratch[pair % 2][:branches, :])):
            own = parted * weight
            other = pltpu.roll(own, branches, 1)
            start = part * both
            for t, (upper, lower) in enumerate(((own, other), (other, own))):
                pair_ref[2 * pair + t, start : start + branches, :] = jnp.where(
                    near, upper, 0.0
                ).astype(BF16)
                pair_ref[2 * pair + t, start + branches : start + both, :] = jnp.where(
                    near, 0.0, lower
                ).astype(BF16)

    for phase in range(group + 1):
        before = phase - 1
        if phase < group:
            third_mixer = mixer(2, phase)
        if phase > 0:
            second_mixer = mixer(1, before)
            total = jnp.zeros((branches, both), F32)
        for at in range(0, branches, 2):
            if phase > 0:
                total = over_j(before, second_mixer, at, total)
            if phase < group:
                over_k(phase, third_mixer, at)
        if phase > 0:
            finish(before, total)


def contract_rest(places, weights, table, first):
    pairs, branches, both = first.shape[:3]
    group = pairs_per_step(pairs)
    stride = both + 9

    return pl.pallas_call(
        functools.partial(second_kernel, stride, group),
        grid_spec=pltpu.PrefetchScalarGridSpec(
            num_scalar_prefetch=2,
            grid=(pairs // group,),
            in_specs=[pl.BlockSpec(memory_space=pltpu.VMEM)]
            + [pl.BlockSpec((group, branches, both, both), lambda s, *places: (s, 0, 0, 0))],
            out_specs=pl.BlockSpec((2 * group, 2 * both, both), lambda s, *places: (s, 0, 0)),
            scratch_shapes=[pltpu.VMEM((branches * stride, both), F32)] * 2,
        ),
        out_shape=jax.ShapeDtypeStruct((2 * pairs, 2 * both, both), BF16),
        compiler_params=pltpu.CompilerParams(vmem_limit_bytes=44 * MIB),
        cost_estimate=pl.CostEstimate(
            flops=16 * pairs * both * both * branches * branches,
            bytes_accessed=2 * pairs * both * both * branches,
            transcendentals=0,
        ),
        name="contract_rest",
    )(places, weights, table, first)


def terms_kernel(columns, start, places, table_ref, pair_ref, *rest):
    out_refs, packed = rest[:-1], rest[-1]
    rows, lanes = packed.shape[1:]
    state = slice(start, start + rows)
    packed[...] = jnp.zeros_like(packed)
    row = lax.broadcasted_iota(jnp.int32, (rows, lanes), 0)
    lane = lax.broadcasted_iota(jnp.int32, (rows, lanes), 1)
    is_rest = (row == columns - rows + 1) & (lane >= lanes // 2)
    for t in range(pair_ref.shape[0]):
        states = jnp.concatenate(
            [table_ref[places[1, t], state], table_ref[places[2, t], state]], 1
        )
        terms = jnp.dot(states, pair_ref[t], preferred_element_type=F32)
        short = terms.astype(BF16).astype(F32)
        terms = jnp.where(is_rest, pltpu.roll(terms - short, 1, 0), terms)
        packed[places[0, t]] = terms.astype(BF16)
    cap = out_refs[0].shape[0]
    for d, out_ref in enumerate(out_refs):
        out_ref[...] = packed[d * cap : (d + 1) * cap]


def coupling_terms(places, table, start, pairs, columns, row_count, row_cap):
    rows, lanes = table.shape[1] - start, table.shape[2]
    return pl.pallas_call(
        functools.partial(terms_kernel, columns, start),
        in_specs=[pl.BlockSpec(memory_space=pltpu.SMEM)]
        + [pl.BlockSpec(memory_space=pltpu.VMEM)] * 2,
        out_specs=[pl.BlockSpec(memory_space=pltpu.VMEM)] * row_count,
        out_shape=[jax.ShapeDtypeStruct((row_cap, rows, lanes), BF16)] * row_count,
        scratch_shapes=[pltpu.VMEM((row_count * row_cap, rows, lanes), BF16)],
        compiler_params=pltpu.CompilerParams(vmem_limit_bytes=16 * MIB),
        name="coupling_terms",
    )(places, table, pairs)


def update_kernel(columns, first, last, codes, queries, *rest):
    row_count = codes.shape[0]
    arrived, rest = rest[:row_count], rest[row_count:]
    state_ref, source_ref, rate_ref = rest[:3]
    new_ref, next_ref, total = rest[3:]
    homes, rows, lanes = state_ref.shape
    total[...] = jnp.zeros_like(total)
    for d in range(row_count):
        for slot in range(codes.shape[1]):
            code = codes[d, slot]
            total[code] += arrived[d][slot].astype(F32)
    coupled = total[1:]
    if first:
        at = columns - rows
        rate = coupled[:, at : at + 1, :] + coupled[:, at + 1 : at + 2, :]
        lane = lax.broadcasted_iota(jnp.int32, rate.shape, 2)
        rate = jnp.where(lane < lanes // 2, pltpu.roll(rate, lanes // 2, 2), rate)
        rate = jnp.broadcast_to(rate + rate_ref[...], (homes, rows, lanes))
    else:
        rate = rate_ref[...]
    new = (1.0 - DAMPING) * state_ref[...] + DAMPING * (source_ref[...] + coupled) / rate
    new_ref[...] = new
    if first:
        next_ref[0][...] = rate
    if not last:
        send_ref = next_ref[-1]
        for slot in range(queries.shape[0]):
            send_ref[slot] = new_ref[queries[slot]].astype(BF16)


def update(codes, queries, arrived, state, source, rate, columns, first, last):
    homes, rows, lanes = state.shape
    outs = [jax.ShapeDtypeStruct(state.shape, F32)]
    if first:
        outs.append(jax.ShapeDtypeStruct(state.shape, F32))
    if not last:
        outs.append(jax.ShapeDtypeStruct((queries.shape[0], rows, lanes), BF16))
    row_count = len(arrived)

    def kernel(codes, queries, *refs):
        ins = refs[: row_count + 3]
        new_ref = refs[row_count + 3]
        more = refs[row_count + 4 : row_count + 3 + len(outs)]
        update_kernel(columns, first, last, codes, queries, *ins, new_ref, more, refs[-1])

    return pl.pallas_call(
        kernel,
        in_specs=[pl.BlockSpec(memory_space=pltpu.SMEM)] * 2
        + [pl.BlockSpec(memory_space=pltpu.VMEM)] * (row_count + 3),
        out_specs=[pl.BlockSpec(memory_space=pltpu.VMEM)] * len(outs),
        out_shape=outs,
        scratch_shapes=[pltpu.VMEM((homes + 1, rows, lanes), F32)],
        compiler_params=pltpu.CompilerParams(vmem_limit_bytes=16 * MIB),
        name="update",
    )(codes, queries, *arrived, state, source, rate)


def body(eigvecs, cubic, triplets, weights, deviation, source, base_rate):
    row_count = lax.axis_size("row")
    devices = lax.axis_size("trip") * row_count
    home_rows, branches = eigvecs.shape[:2]
    trip_local = cubic.shape[0]
    columns = deviation.shape[1] // branches
    far_cap = (2 * trip_local + devices - 1) // devices
    row_cap = trip_local // 2
    rows = 8 * ((columns + 2 + 15) // 16)

    def packed(values):
        values = jnp.swapaxes(values.reshape(home_rows, branches, columns), 1, 2)
        values = jnp.pad(values, ((0, 0), (0, 2 * rows - columns), (0, 0)))
        values = values.reshape(home_rows, 2, rows, branches)
        return jnp.swapaxes(values, 1, 2).reshape(home_rows, rows, 2 * branches)

    def unpacked(values):
        values = jnp.swapaxes(values.reshape(home_rows, rows, 2, branches), 1, 2)
        values = values.reshape(home_rows, 2 * rows, branches)[:, :columns]
        return jnp.swapaxes(values, 1, 2).reshape(home_rows, branches * columns)

    def far(values):
        return lax.all_to_all(values, AXES, split_axis=0, concat_axis=0, tiled=True)

    message, places = prepare(triplets, home_rows, devices, far_cap, row_count, row_cap)
    heard = far(message.reshape(devices, 1, LANES)).reshape(devices, LANES)
    queries = heard[:, :far_cap].reshape(-1)
    asked = lax.dynamic_slice(
        heard, (lax.axis_index("trip") * row_count, far_cap), (row_count, row_cap)
    )
    codes = jnp.take(asked, lax.axis_index("row") ^ jnp.arange(row_count), axis=0, mode="clip")

    state = packed(deviation)
    one = lax.broadcasted_iota(jnp.int32, state.shape[1:], 0) + rows * (
        lax.broadcasted_iota(jnp.int32, state.shape[1:], 1) // branches
    )
    sent_state = jnp.where(one == columns, 1.0, state).astype(BF16)
    records = jnp.concatenate([eigvecs, sent_state], 1)
    far_vecs, near, away = look_up(heard, records, eigvecs, far_cap, row_count, row_cap)
    far_table = far(far_vecs)
    half = row_count // 2
    held = {(r, 0): near[r * row_cap : (r + 1) * row_cap] for r in range(half)}
    sent = [(r, 0) for r in range(half, row_count)]
    moving, bit = away, half
    while bit:
        moved = to_peer(moving, bit, row_count)
        if bit == half:
            source, base_rate, moved = lax.optimization_barrier((source, base_rate, moved))
        for n, (r, o) in enumerate(sent):
            held[r ^ bit, o ^ bit] = moved[n * row_cap : (n + 1) * row_cap]
        bit //= 2
        sent = [key for key in held if key[0] & bit]
        if bit:
            moving = jnp.concatenate([held.pop(key) for key in sent], 0)
    driven = packed(source)
    rate = jnp.concatenate([base_rate, base_rate], 1)[:, None, :]
    first_table = jnp.concatenate([held[0, o] for o in range(row_count)], 0)
    first_table, driven, rate = lax.optimization_barrier((first_table, driven, rate))
    first_part = contract_first(places, first_table, cubic)
    pairs = contract_rest(places, weights, far_table, first_part)

    table, start = far_table, branches
    for step in range(ITERS):
        terms = coupling_terms(places, table, start, pairs, columns, row_count, row_cap)
        arrived = from_peers(terms)
        first, last = step == 0, step == ITERS - 1
        results = update(codes, queries, arrived, state, driven, rate, columns, first, last)
        state = results[0]
        if first:
            rate = results[1]
        if not last:
            table, start = far(results[-1]), 0
    return unpacked(state)


def solution(mesh):
    whole = P(AXES, None, None)
    flat = P(AXES, None)
    in_specs = (whole, whole, flat, P(AXES), flat, flat, flat)
    return jax.shard_map(body, mesh=mesh, in_specs=in_specs, out_specs=flat, check_vma=False)
```

```python
import functools

import jax
import jax.numpy as jnp
from jax import lax
from jax.experimental import pallas as pl
from jax.experimental.pallas import tpu as pltpu
from jax.sharding import PartitionSpec as P

ITERS = 2
DAMPING = 0.7
AXES = ("trip", "row")
F32 = jnp.float32
BF16 = jnp.bfloat16
LANES = 128
MIB = 2**20


def prepare_kernel(home_rows, far_cap, row_count, row_cap, triplets_ref, message_ref, places_ref):
    count, devices = triplets_ref.shape[1], message_ref.shape[0]
    sub = lax.broadcasted_iota(jnp.int32, (count, count), 0)
    lane = lax.broadcasted_iota(jnp.int32, (count, count), 1)
    same, earlier = sub == lane, sub < lane

    def whole_part(values, size):
        return jnp.floor((values.astype(F32) + 0.5) * (1.0 / size)).astype(jnp.int32)

    wanted = [triplets_ref[which : which + 1, :] for which in range(3)]
    owner = [whole_part(values, home_rows) for values in wanted]
    local = [values - own * home_rows for values, own in zip(wanted, owner)]
    upright = [jnp.sum(jnp.where(same, own, 0), 1, keepdims=True) for own in owner]

    def matches(one, two, mask):
        return (mask & (upright[one] == owner[two])).astype(jnp.int32)

    rank = [
        jnp.sum(found, 0, keepdims=True)
        for found in (
            matches(0, 0, earlier),
            matches(1, 1, earlier) + matches(2, 1, earlier),
            matches(1, 2, earlier | same) + matches(2, 2, earlier),
        )
    ]
    device = lax.broadcasted_iota(jnp.int32, (devices, count), 0)
    slot = lax.broadcasted_iota(jnp.int32, (LANES, count), 0)
    kind, precision = (
        (BF16, None) if home_rows <= 256 else (F32, lax.Precision.HIGHEST)
    )
    message = jnp.zeros((devices, LANES), F32)
    for which in range(3):
        value, at = (local[0] + 1, rank[0] + far_cap) if which == 0 else (local[which], rank[which])
        message = message + lax.dot_general(
            jnp.where(device == owner[which], 1.0, 0.0).astype(kind),
            jnp.where(slot == at, value.astype(F32), 0.0).astype(kind),
            (((1,), (1,)), ((), ())),
            precision=precision,
            preferred_element_type=F32,
        )
    message_ref[...] = (message + 0.5).astype(jnp.int32)
    apart = (owner[0] - row_count * whole_part(owner[0], row_count)) ^ lax.axis_index("row")
    places_ref[...] = jnp.zeros_like(places_ref)
    places_ref[0:1, :count] = apart * row_cap + rank[0]
    for which in range(1, 3):
        places_ref[which : which + 1, :count] = owner[which] * far_cap + rank[which]


def prepare(triplets, home_rows, devices, far_cap, row_count, row_cap):
    return pl.pallas_call(
        functools.partial(prepare_kernel, home_rows, far_cap, row_count, row_cap),
        in_specs=[pl.BlockSpec(memory_space=pltpu.VMEM)],
        out_specs=[pl.BlockSpec(memory_space=pltpu.VMEM)] * 2,
        out_shape=[
            jax.ShapeDtypeStruct((devices, LANES), jnp.int32),
            jax.ShapeDtypeStruct((8, LANES), jnp.int32),
        ],
        name="prepare",
    )(triplets.T)


def to_peer(values, bits, count):
    return lax.ppermute(values, "row", [(i, i ^ bits) for i in range(count)])


def from_peers(blocks):
    return [blocks[0]] + [to_peer(blocks[k], k, len(blocks)) for k in range(1, len(blocks))]


def lookup_kernel(far_cap, row_count, heard, record_ref, vec_ref, far_ref, near_ref, away_ref):
    half = row_count // 2
    cap = near_ref.shape[0] // half
    base = lax.axis_index("trip") * row_count
    for k in range(row_count):
        peer = base + (lax.axis_index("row") ^ k)
        row_ref = near_ref if k < half else away_ref
        for slot in range(cap):
            code = heard[peer, far_cap + slot]
            row_ref[k % half * cap + slot] = vec_ref[jnp.maximum(code - 1, 0)]
    for slot in range(far_ref.shape[0]):
        far_ref[slot] = record_ref[heard[slot // far_cap, slot % far_cap]]


def look_up(heard, records, eigvecs, far_cap, row_count, row_cap):
    row_shape = (row_count // 2 * row_cap,) + eigvecs.shape[1:]
    return pl.pallas_call(
        functools.partial(lookup_kernel, far_cap, row_count),
        in_specs=[pl.BlockSpec(memory_space=pltpu.SMEM)]
        + [pl.BlockSpec(memory_space=pltpu.VMEM)] * 2,
        out_specs=[pl.BlockSpec(memory_space=pltpu.VMEM)] * 3,
        out_shape=[
            jax.ShapeDtypeStruct((heard.shape[0] * far_cap,) + records.shape[1:], records.dtype)
        ]
        + [jax.ShapeDtypeStruct(row_shape, eigvecs.dtype)] * 2,
        compiler_params=pltpu.CompilerParams(vmem_limit_bytes=16 * MIB),
        name="look_up",
    )(heard, records, eigvecs)


def pairs_per_step(pairs):
    return next(group for group in (3, 2, 1) if pairs % group == 0)


def first_kernel(cap, offsets, places, *refs):
    vec_refs, (cubic_ref, out_ref) = refs[:-2], refs[-2:]
    group = cubic_ref.shape[0] // 2
    branches = cubic_ref.shape[1]
    both = 2 * branches
    step = 4

    def vectors(t):
        place = places[0, 2 * group * pl.program_id(0) + t]
        block = lax.div(place, cap)
        row = place - block * cap
        found = vec_refs[0][offsets[0] + row]
        for k in range(1, len(vec_refs)):
            found = jnp.where(block == k, vec_refs[k][offsets[k] + row], found)
        return found

    for pair in range(group):
        one, two = vectors(2 * pair), vectors(2 * pair + 1)
        none = jnp.zeros((branches, branches), one.dtype)
        mixer = jnp.concatenate(
            [
                jnp.concatenate([one[:, :branches], none, one[:, branches:], none], 1),
                jnp.concatenate([none, two[:, :branches], none, two[:, branches:]], 1),
            ],
            0,
        )
        for start in range(0, branches, step):
            lanes = slice(start * branches, (start + step) * branches)
            turned = jnp.concatenate(
                [cubic_ref[2 * pair, :, lanes], cubic_ref[2 * pair + 1, :, lanes]], 0
            ).T
            mixed = jnp.dot(turned, mixer, preferred_element_type=F32).astype(BF16)
            for j in range(step):
                for part in range(2):
                    out_ref[pair, start + j, part * branches : (part + 1) * branches] = mixed[
                        j * branches : (j + 1) * branches, part * both : (part + 1) * both
                    ]


def contract_first(places, tables, offsets, cap, cubic):
    count, branches, pairs = cubic.shape
    both = 2 * branches
    group = pairs_per_step(count // 2)

    return pl.pallas_call(
        functools.partial(first_kernel, cap, offsets),
        grid_spec=pltpu.PrefetchScalarGridSpec(
            num_scalar_prefetch=1,
            grid=(count // (2 * group),),
            in_specs=[pl.BlockSpec(memory_space=pltpu.VMEM)] * len(tables)
            + [pl.BlockSpec((2 * group, branches, pairs), lambda s, places: (s, 0, 0))],
            out_specs=pl.BlockSpec((group, branches, both, both), lambda s, places: (s, 0, 0, 0)),
        ),
        out_shape=jax.ShapeDtypeStruct((count // 2, branches, both, both), BF16),
        compiler_params=pltpu.CompilerParams(vmem_limit_bytes=40 * MIB),
        cost_estimate=pl.CostEstimate(
            flops=11 * 2 * count * both * branches * pairs,
            bytes_accessed=2 * count * (both + branches) * pairs,
            transcendentals=0,
        ),
        name="contract_first",
    )(places, *tables, cubic)


def second_kernel(stride, group, places, weights, *refs):
    table_ref, first_ref, pair_ref, *scratch = refs
    branches = first_ref.shape[1]
    both = 2 * branches

    def mixer(which, pair):
        columns = []
        for t in range(2):
            place = places[which, 2 * (group * pl.program_id(0) + pair) + t]
            vectors = table_ref[place, :branches].astype(F32).T
            real, imag = vectors[:branches], vectors[branches:]
            columns += [jnp.concatenate([real, imag], 0), jnp.concatenate([-imag, real], 0)]
        return jnp.concatenate(columns, 1).astype(BF16)

    left = lax.broadcasted_iota(jnp.int32, (both, both), 1) < branches
    none = jnp.zeros((both, both), BF16)

    def apart(block):
        return jnp.concatenate([jnp.where(left, block, none), jnp.where(left, none, block)], 0)

    def over_k(pair, third_mixer, j):
        turned = scratch[pair % 2]
        mixed = jnp.dot(
            third_mixer,
            jnp.concatenate([apart(first_ref[pair, j]), apart(first_ref[pair, j + 1])], 1),
            preferred_element_type=F32,
        )
        for half in range(2):
            for part in range(2):
                turned[pl.ds(part * branches + j + half, branches, stride=stride), :] = mixed[
                    part * branches : (part + 1) * branches, half * both : (half + 1) * both
                ]

    def over_j(pair, second_mixer, c, total):
        turned = scratch[pair % 2]
        columns = [
            apart(turned[(c + half) * stride : (c + half) * stride + both, :].astype(BF16))
            for half in range(2)
        ]
        values = jnp.dot(second_mixer, jnp.concatenate(columns, 1), preferred_element_type=F32)
        real, imag = values[:branches], values[branches:]
        power = real * real + imag * imag
        over_b = jnp.sum(power, 0, keepdims=True)
        for half in range(2):
            lanes = slice(half * both, (half + 1) * both)
            total = total + power[:, lanes]
            turned[pl.ds(c + half, 1), :] = over_b[:, lanes]
        return total

    def finish(pair, total):
        first = 2 * (group * pl.program_id(0) + pair)
        near = left[:branches]
        weight = jnp.where(near, weights[first].astype(F32), weights[first + 1].astype(F32))
        for part, parted in enumerate((total, scratch[pair % 2][:branches, :])):
            own = parted * weight
            other = pltpu.roll(own, branches, 1)
            start = part * both
            for t, (upper, lower) in enumerate(((own, other), (other, own))):
                pair_ref[2 * pair + t, start : start + branches, :] = jnp.where(
                    near, upper, 0.0
                ).astype(BF16)
                pair_ref[2 * pair + t, start + branches : start + both, :] = jnp.where(
                    near, 0.0, lower
                ).astype(BF16)

    for phase in range(group + 1):
        before = phase - 1
        if phase < group:
            third_mixer = mixer(2, phase)
        if phase > 0:
            second_mixer = mixer(1, before)
            total = jnp.zeros((branches, both), F32)
        for at in range(0, branches, 2):
            if phase > 0:
                total = over_j(before, second_mixer, at, total)
            if phase < group:
                over_k(phase, third_mixer, at)
        if phase > 0:
            finish(before, total)


def contract_rest(places, weights, table, first):
    pairs, branches, both = first.shape[:3]
    group = pairs_per_step(pairs)
    stride = both + 9

    return pl.pallas_call(
        functools.partial(second_kernel, stride, group),
        grid_spec=pltpu.PrefetchScalarGridSpec(
            num_scalar_prefetch=2,
            grid=(pairs // group,),
            in_specs=[pl.BlockSpec(memory_space=pltpu.VMEM)]
            + [pl.BlockSpec((group, branches, both, both), lambda s, *places: (s, 0, 0, 0))],
            out_specs=pl.BlockSpec((2 * group, 2 * both, both), lambda s, *places: (s, 0, 0)),
            scratch_shapes=[pltpu.VMEM((branches * stride, both), F32)] * 2,
        ),
        out_shape=jax.ShapeDtypeStruct((2 * pairs, 2 * both, both), BF16),
        compiler_params=pltpu.CompilerParams(vmem_limit_bytes=44 * MIB),
        cost_estimate=pl.CostEstimate(
            flops=16 * pairs * both * both * branches * branches,
            bytes_accessed=2 * pairs * both * both * branches,
            transcendentals=0,
        ),
        name="contract_rest",
    )(places, weights, table, first)


def terms_kernel(columns, start, places, table_ref, pair_ref, *rest):
    out_refs, packed = rest[:-1], rest[-1]
    rows, lanes = packed.shape[1:]
    state = slice(start, start + rows)
    packed[...] = jnp.zeros_like(packed)
    row = lax.broadcasted_iota(jnp.int32, (rows, lanes), 0)
    lane = lax.broadcasted_iota(jnp.int32, (rows, lanes), 1)
    is_rest = (row == columns - rows + 1) & (lane >= lanes // 2)
    for t in range(pair_ref.shape[0]):
        states = jnp.concatenate(
            [table_ref[places[1, t], state], table_ref[places[2, t], state]], 1
        )
        terms = jnp.dot(states, pair_ref[t], preferred_element_type=F32)
        short = terms.astype(BF16).astype(F32)
        terms = jnp.where(is_rest, pltpu.roll(terms - short, 1, 0), terms)
        packed[places[0, t]] = terms.astype(BF16)
    cap = out_refs[0].shape[0]
    for d, out_ref in enumerate(out_refs):
        out_ref[...] = packed[d * cap : (d + 1) * cap]


def coupling_terms(places, table, start, pairs, columns, row_count, row_cap):
    rows, lanes = table.shape[1] - start, table.shape[2]
    return pl.pallas_call(
        functools.partial(terms_kernel, columns, start),
        in_specs=[pl.BlockSpec(memory_space=pltpu.SMEM)]
        + [pl.BlockSpec(memory_space=pltpu.VMEM)] * 2,
        out_specs=[pl.BlockSpec(memory_space=pltpu.VMEM)] * row_count,
        out_shape=[jax.ShapeDtypeStruct((row_cap, rows, lanes), BF16)] * row_count,
        scratch_shapes=[pltpu.VMEM((row_count * row_cap, rows, lanes), BF16)],
        compiler_params=pltpu.CompilerParams(vmem_limit_bytes=16 * MIB),
        name="coupling_terms",
    )(places, table, pairs)


def update_kernel(columns, first, last, codes, queries, *rest):
    row_count = codes.shape[0]
    arrived, rest = rest[:row_count], rest[row_count:]
    state_ref, source_ref, rate_ref = rest[:3]
    new_ref, next_ref, total = rest[3:]
    homes, rows, lanes = state_ref.shape
    total[...] = jnp.zeros_like(total)
    for d in range(row_count):
        for slot in range(codes.shape[1]):
            code = codes[d, slot]
            total[code] += arrived[d][slot].astype(F32)
    coupled = total[1:]
    if first:
        at = columns - rows
        rate = coupled[:, at : at + 1, :] + coupled[:, at + 1 : at + 2, :]
        lane = lax.broadcasted_iota(jnp.int32, rate.shape, 2)
        rate = jnp.where(lane < lanes // 2, pltpu.roll(rate, lanes // 2, 2), rate)
        rate = jnp.broadcast_to(rate + rate_ref[...], (homes, rows, lanes))
    else:
        rate = rate_ref[...]
    new = (1.0 - DAMPING) * state_ref[...] + DAMPING * (source_ref[...] + coupled) / rate
    new_ref[...] = new
    if first:
        next_ref[0][...] = rate
    if not last:
        send_ref = next_ref[-1]
        for slot in range(queries.shape[0]):
            send_ref[slot] = new_ref[queries[slot]].astype(BF16)


def update(codes, queries, arrived, state, source, rate, columns, first, last):
    homes, rows, lanes = state.shape
    outs = [jax.ShapeDtypeStruct(state.shape, F32)]
    if first:
        outs.append(jax.ShapeDtypeStruct(state.shape, F32))
    if not last:
        outs.append(jax.ShapeDtypeStruct((queries.shape[0], rows, lanes), BF16))
    row_count = len(arrived)

    def kernel(codes, queries, *refs):
        ins = refs[: row_count + 3]
        new_ref = refs[row_count + 3]
        more = refs[row_count + 4 : row_count + 3 + len(outs)]
        update_kernel(columns, first, last, codes, queries, *ins, new_ref, more, refs[-1])

    return pl.pallas_call(
        kernel,
        in_specs=[pl.BlockSpec(memory_space=pltpu.SMEM)] * 2
        + [pl.BlockSpec(memory_space=pltpu.VMEM)] * (row_count + 3),
        out_specs=[pl.BlockSpec(memory_space=pltpu.VMEM)] * len(outs),
        out_shape=outs,
        scratch_shapes=[pltpu.VMEM((homes + 1, rows, lanes), F32)],
        compiler_params=pltpu.CompilerParams(vmem_limit_bytes=16 * MIB),
        name="update",
    )(codes, queries, *arrived, state, source, rate)


def body(eigvecs, cubic, triplets, weights, deviation, source, base_rate):
    row_count = lax.axis_size("row")
    devices = lax.axis_size("trip") * row_count
    home_rows, branches = eigvecs.shape[:2]
    trip_local = cubic.shape[0]
    columns = deviation.shape[1] // branches
    far_cap = (2 * trip_local + devices - 1) // devices
    row_cap = trip_local // 2
    rows = 8 * ((columns + 2 + 15) // 16)

    def packed(values):
        values = jnp.swapaxes(values.reshape(home_rows, branches, columns), 1, 2)
        values = jnp.pad(values, ((0, 0), (0, 2 * rows - columns), (0, 0)))
        values = values.reshape(home_rows, 2, rows, branches)
        return jnp.swapaxes(values, 1, 2).reshape(home_rows, rows, 2 * branches)

    def unpacked(values):
        values = jnp.swapaxes(values.reshape(home_rows, rows, 2, branches), 1, 2)
        values = values.reshape(home_rows, 2 * rows, branches)[:, :columns]
        return jnp.swapaxes(values, 1, 2).reshape(home_rows, branches * columns)

    def far(values):
        return lax.all_to_all(values, AXES, split_axis=0, concat_axis=0, tiled=True)

    message, places = prepare(triplets, home_rows, devices, far_cap, row_count, row_cap)
    heard = far(message.reshape(devices, 1, LANES)).reshape(devices, LANES)
    queries = heard[:, :far_cap].reshape(-1)
    asked = lax.dynamic_slice(
        heard, (lax.axis_index("trip") * row_count, far_cap), (row_count, row_cap)
    )
    codes = jnp.take(asked, lax.axis_index("row") ^ jnp.arange(row_count), axis=0, mode="clip")

    state = packed(deviation)
    one = lax.broadcasted_iota(jnp.int32, state.shape[1:], 0) + rows * (
        lax.broadcasted_iota(jnp.int32, state.shape[1:], 1) // branches
    )
    sent_state = jnp.where(one == columns, 1.0, state).astype(BF16)
    records = jnp.concatenate([eigvecs, sent_state], 1)
    far_vecs, near, away = look_up(heard, records, eigvecs, far_cap, row_count, row_cap)
    far_table = far(far_vecs)
    half = row_count // 2
    held = {(r, 0): (near, r * row_cap) for r in range(half)}
    sent = [(r, 0) for r in range(half, row_count)]
    moving, bit = away, half
    while bit:
        moved = to_peer(moving, bit, row_count)
        if bit == half:
            source, base_rate, moved = lax.optimization_barrier((source, base_rate, moved))
        for n, (r, o) in enumerate(sent):
            held[r ^ bit, o ^ bit] = (moved, n * row_cap)
        bit //= 2
        sent = [key for key in held if key[0] & bit]
        if bit:
            parts = [held.pop(key) for key in sent]
            moving = jnp.concatenate([v[start : start + row_cap] for v, start in parts], 0)
    driven = packed(source)
    rate = jnp.concatenate([base_rate, base_rate], 1)[:, None, :]
    tables, offsets = zip(*[held[0, o] for o in range(row_count)])
    tables, driven, rate = lax.optimization_barrier((tables, driven, rate))
    first_part = contract_first(places, tables, offsets, row_cap, cubic)
    pairs = contract_rest(places, weights, far_table, first_part)

    table, start = far_table, branches
    for step in range(ITERS):
        terms = coupling_terms(places, table, start, pairs, columns, row_count, row_cap)
        arrived = from_peers(terms)
        first, last = step == 0, step == ITERS - 1
        results = update(codes, queries, arrived, state, driven, rate, columns, first, last)
        state = results[0]
        if first:
            rate = results[1]
        if not last:
            table, start = far(results[-1]), 0
    return unpacked(state)


def solution(mesh):
    whole = P(AXES, None, None)
    flat = P(AXES, None)
    in_specs = (whole, whole, flat, P(AXES), flat, flat, flat)
    return jax.shard_map(body, mesh=mesh, in_specs=in_specs, out_specs=flat, check_vma=False)
```
